32 devices in a mesh: gx: 4 (over y, x), gy: 4 (over z), gz: 2 (over core).
Axes of the slice: x: 2, y: 2, z: 4, core: 2. Of those that a mesh axis runs over, the one named last changes fastest.
Arguments:
- theta_field: float32 [4, 4, 128, 12288], P('gx', 'gy', 'gz'), may hold values from -6 to 6
- courants: bfloat16 [3, 4, 4, 128, 12288], P(None, 'gx', 'gy', 'gz'), may hold values from -0.27929688 to 0.27929688
- meso_columns: float32 [60, 32768], P(None, ('gx', 'gy', 'gz')), may hold values from -6 to 6
- col_weight: float32 [32768], P(('gx', 'gy', 'gz')), may hold values from 0.25 to 1
- owner_ids: int32 [32768, 1], P(('gx', 'gy', 'gz')), may hold values from 0 to 7; in each aligned block of 1024 rows (0 to 1023, 1024 to 2047, ...) at most 384 rows name the same one
- line_ids: int32 [32768], P(('gx', 'gy', 'gz')), may hold values from 0 to 767
- band_start: int32 [32768], P(('gx', 'gy', 'gz')), may hold values from 0 to 11
Outputs:
- theta_next: float32 [4, 4, 128, 12288], P('gx', 'gy', 'gz')
The draws below stay inside these ranges and needn't reach their ends.
Inputs may be any that keep to these rules, and one draw needn't show every extreme that they name: `owner_ids`: owner o is fringe side o mod 2 of y tile o div 2. Among the rows of one device no owner appears more than 384 times, and some owner appears exactly 384 times.
All inputs are finite; a program needn't handle non-finite values.
Results may differ from the reference program's by a relative error of at most 0.00059.
Values may be sent and summed in bfloat16 or wider, within the bound.
A program may use at most 128 MiB of HBM per device.

```python
import math
import jax
import jax.numpy as jnp
import numpy as np
from jax import lax

CX = 16
NY = 3072
ZG = 128
LEV = 60
KM = 64
FW = 8
NSTEP = 4
COL_DEV = 1024
NX = 64
CY = 768
CAP = 384
COLS = 32768
N_GX = 4
N_GY = 4


def touch_ends(entries, own_key, low, largest):
    longest = entries.shape.index(max(entries.shape))
    spots = []
    for shift in (0, 1):
        where = [jax.random.randint(jax.random.fold_in(own_key, axis), (), 0, length) for axis, length in enumerate(entries.shape)]
        where[longest] = (where[longest] + shift) % entries.shape[longest]
        spots.append(tuple(where))
    return entries.at[spots[0]].set(low).at[spots[1]].set(largest)


def shard_levels(rng, extent, split, smallest, top_value):
    factor_of = 1.0
    for axis_at, shards_of in split:
        steps = jax.random.uniform(jax.random.fold_in(jax.random.fold_in(rng, 6), axis_at), (shards_of,), jnp.float32, smallest / len(split), top_value / len(split))
        factor_of = factor_of * jnp.repeat(jnp.exp(steps), extent[axis_at] // shards_of).reshape((-1,) + (1,) * (len(extent) - 1 - axis_at))
    return factor_of


def deal_out(rng, own, number, rows, number_of, top, limit, slope):
    ranking = jax.random.permutation(rng, number_of)
    crowded, usual = shares(number_of, rows * top, limit, slope, True), shares(number_of, rows * top, limit, slope, False)
    places = jnp.arange(number_of)

    def named(sizes, turn):
        used = int((sizes > 0).sum())
        fixed = max(1, used // 4)
        passed = fixed + (places - fixed + turn * (used - fixed)) % max(1, number_of - fixed)
        return jnp.zeros((number_of,), jnp.int32).at[ranking[jnp.where(places < fixed, places, passed)]].set(jnp.asarray(sizes, jnp.int32))

    sizes = jnp.where(number % 4 == 0, named(crowded, number // 4), named(usual, number - number // 4 - 1))
    mixed = jax.random.permutation(jax.random.fold_in(own, 3), number_of)
    source_of, receiver = mixed[0:number_of // 2 * 2:2], mixed[1:number_of // 2 * 2:2]
    margin = jnp.minimum(sizes[source_of] - 1, limit - sizes[receiver]) // 2
    margin = jnp.where((source_of == ranking[0]) | (receiver == ranking[0]) | (sizes[receiver] == 0), 0, jnp.maximum(margin, 0))
    passed = jax.random.randint(jax.random.fold_in(own, 4), (number_of // 2,), 0, 1 << 20) % (margin + 1)
    sizes = sizes.at[source_of].add(-passed).at[receiver].add(passed)
    members = jnp.searchsorted(jnp.cumsum(sizes), jnp.arange(rows * top), side="right").astype(jnp.int32)
    table = members.reshape(top, rows).T
    table = table[jax.random.permutation(jax.random.fold_in(own, 1), rows)]
    turn = jax.random.randint(jax.random.fold_in(own, 2), (rows, 1), 0, top)
    return jnp.take_along_axis(table, (jnp.arange(top)[None, :] + turn) % top, axis=1)


def shares(amount, total, most, lean, full):
    weights = [(1 << 20) // math.isqrt(standing ** lean) + 1 for standing in range(1, amount + 1)]
    largest = most if full else min(most, max(-(-total // amount), total * weights[0] // sum(weights)))
    least = 1 if total - largest >= amount - 1 else 0
    counts, surplus = [largest] + [least] * (amount - 1), total - largest - least * (amount - 1)
    while surplus > 0:
        movable = [i for i in range(1, amount) if counts[i] < largest] or [i for i in range(1, amount) if counts[i] < most]
        pool, remaining = sum([weights[i] for i in movable]), surplus
        for i in movable:
            extra = min(most - counts[i], max(1, remaining * weights[i] // pool), surplus)
            counts[i] = counts[i] + extra
            surplus = surplus - extra
    return np.array(counts)


def bell_draw(own_key, dims, width, limit, pieces=(), kind=jnp.bfloat16):
    array = width * jax.random.normal(own_key, dims, jnp.float32)
    if pieces:
        array = array * shard_levels(own_key, dims, pieces, -0.22, 0.18)
    return jnp.clip(array, -limit, limit).astype(kind)


def setup_inputs(seed: int = 0) -> dict:
    splits = jax.random.split(jax.random.key(seed), 8)
    theta_field = bell_draw(splits[0], (N_GX, N_GY, ZG, CX * CY), 1.0, 6.0, ((0, 4), (1, 4), (2, 2)), jnp.float32)
    courants = jnp.clip(jax.random.uniform(splits[1], (3, N_GX, N_GY, ZG, CX * CY), jnp.float32, -0.27929688, 0.27929688) * shard_levels(splits[1], (3, N_GX, N_GY, ZG, CX * CY), ((1, 4), (2, 4), (3, 2)), -0.4, 0.0), -0.27929688, 0.27929688).astype(jnp.bfloat16)
    meso_columns = bell_draw(splits[2], (LEV, COLS), 1.0, 6.0, ((1, 32),), jnp.float32)
    col_weight = jnp.clip(jnp.exp(math.log(1.0) - 1.3862944 * jax.random.uniform(splits[3], (COLS,), jnp.float32) ** shard_levels(splits[3], (COLS,), ((0, 32),), -0.2, 0.2)), 0.25, 1.0)
    owner_ids_keys = jax.random.split(jax.random.fold_in(splits[4], 1), COLS // COL_DEV)
    owner_ids_turns = jax.random.permutation(jax.random.fold_in(splits[4], 3), COLS // COL_DEV)
    owner_ids = jax.vmap(lambda own, number: deal_out(jax.random.fold_in(splits[4], 2), own, number, COL_DEV, 2 * N_GY, 1, CAP, 2))(owner_ids_keys, owner_ids_turns).reshape((COLS, 1))
    line_ids = touch_ends(jax.random.randint(splits[5], (COLS,), 0, CY), jax.random.fold_in(splits[5], 1), 0, CY - 1).astype(jnp.int32)
    band_start = touch_ends(jax.random.randint(splits[6], (COLS,), 0, LEV - 3 * (ZG - 1) // 8 - 1), jax.random.fold_in(splits[6], 1), 0, (LEV - 3 * (ZG - 1) // 8 - 1) - 1).astype(jnp.int32)
    return dict(theta_field=theta_field, courants=courants, meso_columns=meso_columns, col_weight=col_weight, owner_ids=owner_ids, line_ids=line_ids, band_start=band_start)


diffusion = 0.02


def band_lookup():
    levels_z = jnp.arange(ZG, dtype=jnp.int32)
    lower_index = (3 * levels_z) // 8
    fraction = ((3 * levels_z) % 8).astype(jnp.float32) / 8.0
    return lower_index, fraction


def wave_table(first_row, row_count):
    places = first_row + jnp.arange(row_count, dtype=jnp.int32)
    numbers = jnp.arange(KM, dtype=jnp.int32)
    phases = (places[:, None] * numbers[None, :]) % NY
    angles = phases.astype(jnp.float32) * (2.0 * math.pi / NY)
    return jnp.concatenate([jnp.cos(angles), jnp.sin(angles)], axis=1)


def mode_scale():
    return jnp.where(jnp.arange(2 * KM, dtype=jnp.int32) % KM == 0, 1.0 / NY, 2.0 / NY).astype(jnp.float32)


def upwind(state_field, courant_one, ahead_cell, behind_cell):
    return -jnp.maximum(courant_one, 0.0) * (state_field - behind_cell) - jnp.minimum(courant_one, 0.0) * (ahead_cell - state_field)


def advance(state_field, courants, ahead_x, behind_x, ahead_z, behind_z, ahead_y, behind_y):
    change = upwind(state_field, courants[0].astype(jnp.float32), ahead_x, behind_x)
    change = change + upwind(state_field, courants[1].astype(jnp.float32), ahead_z, behind_z)
    change = change + upwind(state_field, courants[2].astype(jnp.float32), ahead_y, behind_y)
    neighbours = ahead_x + behind_x + ahead_z + behind_z + ahead_y + behind_y
    return state_field + change + diffusion * (neighbours - 6.0 * state_field)


def sweep_once(state_field, courants):
    zero_layer = jnp.zeros_like(state_field[:, :1])
    ahead_z = jnp.concatenate([state_field[:, 1:], zero_layer], axis=1)
    behind_z = jnp.concatenate([zero_layer, state_field[:, :-1]], axis=1)
    return advance(state_field, courants, jnp.roll(state_field, -1, axis=0), jnp.roll(state_field, 1, axis=0), ahead_z, behind_z, jnp.roll(state_field, -1, axis=2), jnp.roll(state_field, 1, axis=2))


def to_grid(blocked):
    tiles_x = blocked.shape[0]
    tiles_y = blocked.shape[1]
    levels = blocked.shape[2]
    shaped = blocked.reshape(tiles_x, tiles_y, levels, CX, CY)
    return shaped.transpose(0, 3, 2, 1, 4).reshape(tiles_x * CX, levels, tiles_y * CY)


def to_blocks(grid):
    tiles_x = grid.shape[0] // CX
    tiles_y = grid.shape[2] // CY
    levels = grid.shape[1]
    shaped = grid.reshape(tiles_x, CX, levels, tiles_y, CY)
    return shaped.transpose(0, 3, 2, 1, 4).reshape(tiles_x, tiles_y, levels, CX * CY)


def reference(theta_field, courants, meso_columns, col_weight, owner_ids, line_ids, band_start):
    theta_grid = to_grid(theta_field)
    courant_grid = jnp.stack([to_grid(courants[0]), to_grid(courants[1]), to_grid(courants[2])])
    lower_index, fraction = band_lookup()
    column_major = meso_columns.T
    index_low = (band_start[:, None] + lower_index[None, :]).astype(jnp.int32)
    below_level = jnp.take_along_axis(column_major, index_low, axis=1)
    above_level = jnp.take_along_axis(column_major, index_low + 1, axis=1)
    profile = (1.0 - fraction)[None, :] * below_level + fraction[None, :] * above_level
    weighted = profile * col_weight[:, None]
    owners = owner_ids[:, 0]
    target_row = ((owners % 2) * NY + (owners // 2) * CY + line_ids).astype(jnp.int32)
    target = jax.ops.segment_sum(weighted, target_row, num_segments=2 * NY)
    target = target.reshape(2, NY, ZG).transpose(0, 2, 1)
    west_strip = theta_grid[:FW]
    east_strip = theta_grid[NX - FW:]
    gap_strip = jnp.concatenate([(target[0][None] - west_strip).astype(jnp.bfloat16), (target[1][None] - east_strip).astype(jnp.bfloat16)], axis=0)
    wave_basis = wave_table(0, NY)
    spectrum = jnp.einsum('xky,ym->xkm', gap_strip.astype(jnp.float32), wave_basis, precision=lax.Precision.HIGHEST)
    smooth = jnp.einsum('xkm,ym->xky', spectrum * mode_scale()[None, None, :], wave_basis, precision=lax.Precision.HIGHEST)
    offsets = jnp.arange(FW, dtype=jnp.float32)
    relax_west = (FW - offsets) / FW
    relax_east = (offsets + 1.0) / FW
    nudged = theta_grid.at[:FW].add(relax_west[:, None, None] * smooth[:FW])
    nudged = nudged.at[NX - FW:].add(relax_east[:, None, None] * smooth[FW:])
    state_field = nudged
    for step_index in range(NSTEP):
        state_field = sweep_once(state_field, courant_grid)
    return to_blocks(state_field)
```

```python
import functools
import math

import jax
import jax.numpy as jnp
from jax import lax
from jax.experimental import pallas as pl
from jax.experimental.pallas import tpu as pltpu
from jax.sharding import PartitionSpec as P

CX = 16
NY = 3072
ZG = 128
KM = 64
FW = 8
NSTEP = 4
LANES = 128
ROWS = 8

MESH = pl.DeviceIdType.MESH
diffusion = 0.02
highest = lax.Precision.HIGHEST
band_span = 3 * (ZG - 1) // 8 + 2


def extended(array, sides, width, wrap):
    for axis, dim in sides:
        devices, length = (lax.axis_size(axis), array.shape[dim])
        up = [(i, (i + 1) % devices) for i in range(devices if wrap else devices - 1)]
        down = [(j, i) for i, j in up]
        last = lax.slice_in_dim(array, length - width, length, axis=dim)
        initial = lax.slice_in_dim(array, 0, width, axis=dim)
        before = lax.ppermute(last, axis, up)
        after = lax.ppermute(initial, axis, down)
        array = jnp.concatenate([before, array, after], axis=dim)
    return array


def band_matrix():
    levels_z = jnp.arange(ZG, dtype=jnp.int32)
    lower_index = 3 * levels_z // 8
    fraction = (3 * levels_z % 8).astype(jnp.float32) / 8.0
    entries = jnp.arange(band_span, dtype=jnp.int32)[None, :]
    return (1.0 - fraction)[:, None] * (entries == lower_index[:, None]) + fraction[:, None] * (
        entries == lower_index[:, None] + 1
    )


def waves_at(places):
    numbers = jnp.arange(KM, dtype=jnp.int32)
    phases = places[:, None] * numbers[None, :] % NY
    angles = phases.astype(jnp.float32) * (2.0 * math.pi / NY)
    return jnp.concatenate([jnp.cos(angles), jnp.sin(angles)], axis=1)


def mode_scale():
    return jnp.where(jnp.arange(2 * KM, dtype=jnp.int32) % KM == 0, 1.0 / NY, 2.0 / NY).astype(
        jnp.float32
    )


def upwind(state_field, courant_one, ahead_cell, behind_cell):
    return -jnp.maximum(courant_one, 0.0) * (state_field - behind_cell) - jnp.minimum(
        courant_one, 0.0
    ) * (ahead_cell - state_field)


def sweep_once(state_field, courant_local):
    side_cells = extended(state_field, (("gx", 1), ("gy", 2)), 1, True)
    level_cells = extended(state_field, (("gz", 0),), 1, False)
    pairs = (
        (side_cells[:, 2:, 1:-1], side_cells[:, :-2, 1:-1]),
        (level_cells[2:], level_cells[:-2]),
        (side_cells[:, 1:-1, 2:], side_cells[:, 1:-1, :-2]),
    )
    change = 0.0
    neighbours = 0.0
    for direction, (ahead, behind) in enumerate(pairs):
        change = change + upwind(
            state_field, courant_local[direction].astype(jnp.float32), ahead, behind
        )
        neighbours = neighbours + ahead + behind
    return state_field + change + diffusion * (neighbours - 6.0 * state_field)


def target_spectrum(meso_columns, col_weight, owner_ids, line_ids, band_start, tile_rows):
    owners = owner_ids[:, 0]
    places = owners // 2 * tile_rows + line_ids
    waves = waves_at(places) * col_weight[:, None]
    sided = jnp.concatenate(
        [jnp.where((owners % 2 == side)[:, None], waves, 0.0) for side in range(2)], axis=1
    )
    shifted = jnp.zeros((band_span, meso_columns.shape[1]), jnp.float32)
    for offset in range(meso_columns.shape[0] - band_span + 1):
        shifted = shifted + jnp.where(
            band_start[None, :] == offset, meso_columns[offset : offset + band_span], 0.0
        )
    return jnp.dot(shifted, sided, precision=highest, preferred_element_type=jnp.float32)


def sweep_kernel(
    sizes,
    theta_ref,
    courant_ref,
    coef_ref,
    waves_ref,
    out_ref,
    state,
    weight,
    courant,
    coef,
    waves,
    x_send,
    x_recv,
    y_send,
    y_recv,
    in_sem,
    out_sem,
    xs_sem,
    xr_sem,
    ys_sem,
    yr_sem,
    zs_sem,
    zr_sem,
):
    n_gx, n_gy, levels, tiles = sizes
    chunks = levels // ROWS
    planes = CX * tiles
    gx, gy, gz = (lax.axis_index(axis) for axis in ("gx", "gy", "gz"))
    x_right, x_left = lax.rem(gx + 1, n_gx), lax.rem(gx + n_gx - 1, n_gx)
    y_right, y_left = lax.rem(gy + 1, n_gy), lax.rem(gy + n_gy - 1, n_gy)
    other = 1 - gz
    east_end = gx == n_gx - 1
    west_end = gx == 0
    body_rows = pl.ds(ROWS, levels)

    def tile_lanes(tile):
        return pl.ds(pl.multiple_of(tile * LANES, LANES), LANES)

    courant_copy = pltpu.make_async_copy(courant_ref, courant, in_sem.at[1])
    coef_copy = pltpu.make_async_copy(coef_ref, coef, in_sem.at[2])
    waves_copy = pltpu.make_async_copy(waves_ref, waves, in_sem.at[3])

    def fetch(tile, carry):
        pltpu.make_async_copy(
            theta_ref.at[:, tile_lanes(tile)],
            state.at[0, tile + tiles, body_rows, :],
            in_sem.at[0],
        ).start()
        return carry

    courant_copy.start()
    lax.fori_loop(0, planes, fetch, 0)
    coef_copy.start()
    waves_copy.start()

    barrier = pltpu.get_barrier_semaphore()
    neighbours = (
        {"gx": x_right},
        {"gx": x_left},
        {"gy": y_right},
        {"gy": y_left},
        {"gz": other},
    )
    for neighbour in neighbours:
        pl.semaphore_signal(barrier, inc=1, device_id=neighbour, device_id_type=MESH)

    zero_rows = pl.ds(pl.multiple_of(jnp.where(gz == 0, 0, ROWS + levels), ROWS), ROWS)

    def blank(tile, carry):
        for buffer in range(2):
            state[buffer, tile + tiles, zero_rows, :] = jnp.zeros((ROWS, LANES), jnp.float32)
        return carry

    lax.fori_loop(0, planes, blank, 0)
    y_send[...] = jnp.zeros_like(y_send)
    lane = lax.broadcasted_iota(jnp.int32, (ROWS, LANES), 1)

    courant_copy.wait()

    def weigh(tile, carry):
        centre = 1.0
        for direction in range(3):
            number = courant[direction, :, tile_lanes(tile)].astype(jnp.float32)
            upward = jnp.maximum(number, 0.0)
            behind = upward + diffusion
            ahead = (upward - number) + diffusion
            weight[2 * direction + 1, tile] = behind
            weight[2 * direction + 2, tile] = ahead
            centre = centre - (behind + ahead)
        weight[0, tile] = centre
        return carry

    lax.fori_loop(0, planes, weigh, 0)

    whole = state.at[0, pl.ds(tiles, planes), body_rows, :]
    pltpu.make_async_copy(whole, whole, in_sem.at[0]).wait()
    coef_copy.wait()
    waves_copy.wait()

    @pl.when(jnp.logical_or(west_end, east_end))
    def _():
        first = jnp.where(east_end, CX - FW, 0)

        def nudge(index, carry):
            smooth = jnp.dot(
                coef[index], waves[...], precision=highest, preferred_element_type=jnp.float32
            )
            base = (first + index + 1) * tiles
            for tile in range(tiles):
                state[0, base + tile, body_rows, :] += smooth[:, tile * LANES : (tile + 1) * LANES]
            return carry

        lax.fori_loop(0, FW, nudge, 0)

    source_rows = pl.ds(pl.multiple_of(jnp.where(gz == 0, levels, ROWS), ROWS), ROWS)
    target_rows = pl.ds(pl.multiple_of(jnp.where(gz == 0, 0, ROWS + levels), ROWS), ROWS)

    def z_copy(step, group, first, count):
        buffer = lax.rem(step, 2)
        some = pl.ds((first + 1) * tiles, count * tiles)
        return pltpu.make_async_remote_copy(
            src_ref=state.at[buffer, some, source_rows, :],
            dst_ref=state.at[buffer, some, target_rows, :],
            send_sem=zs_sem.at[step, group],
            recv_sem=zr_sem.at[step, group],
            device_id={"gz": other},
            device_id_type=MESH,
        )

    def y_copy(step, group, side):
        return pltpu.make_async_remote_copy(
            src_ref=y_send.at[step, group, side],
            dst_ref=y_recv.at[step, group, side],
            send_sem=ys_sem.at[step, group, side],
            recv_sem=yr_sem.at[step, group, side],
            device_id={"gy": y_right if side == 0 else y_left},
            device_id_type=MESH,
        )

    def x_copy(step, side):
        return pltpu.make_async_remote_copy(
            src_ref=x_send.at[step, side],
            dst_ref=x_recv.at[step, side],
            send_sem=xs_sem.at[step, side],
            recv_sem=xr_sem.at[step, side],
            device_id={"gx": x_right if side == 0 else x_left},
            device_id_type=MESH,
        )

    half = (CX - 2) // 2
    groups = ((1, half), (1 + half, half), (0, 1), (CX - 1, 1))

    def pack(step, group, plane, chunk, low, high):
        place = plane + chunk * CX
        here = lane == place
        y_send[step, group, 0] = jnp.where(
            here, pltpu.roll(high, lax.rem(place + 1, LANES), 1), y_send[step, group, 0]
        )
        y_send[step, group, 1] = jnp.where(
            here, pltpu.roll(low, place, 1), y_send[step, group, 1]
        )

    def send(step, group):
        z_copy(step, group, *groups[group]).start()
        for side in range(2):
            y_copy(step, group, side).start()
        if group >= 2:
            side = 3 - group
            buffer = lax.rem(step, 2)
            base = (groups[group][0] + 1) * tiles
            for tile in range(tiles):
                x_send[step, side, tile] = state[buffer, base + tile, body_rows, :].astype(
                    jnp.bfloat16
                )
            x_copy(step, side).start()

    pl.semaphore_wait(barrier, len(neighbours))

    def plane_of(turn):
        plane = jnp.where(turn < 2 * half, turn + 1, jnp.where(turn == 2 * half, 0, CX - 1))
        group = jnp.where(
            turn < half, 0, jnp.where(turn < 2 * half, 1, jnp.where(turn == 2 * half, 2, 3))
        )
        return plane, group

    def pack_start(turn, carry):
        plane, group = plane_of(turn)
        base = (plane + 1) * tiles
        for chunk in range(chunks):
            rows = pl.ds(ROWS + chunk * ROWS, ROWS)
            pack(
                0, group, plane, chunk, state[0, base, rows, :], state[0, base + tiles - 1, rows, :]
            )
        return carry

    lax.fori_loop(0, CX, pack_start, 0)
    for group in (2, 3, 0, 1):
        send(jnp.int32(0), group)

    starts = (0, half, 2 * half, 2 * half + 1)

    def advance(step, carry):
        now = lax.rem(step, 2)
        later = 1 - now

        def one(turn, carry):
            plane, group = plane_of(turn)
            for which in range(4):

                @pl.when(turn == starts[which])
                def _():
                    z_copy(step, which, *groups[which]).wait_recv()
                    for side in range(2):
                        y_copy(step, which, side).wait_recv()

                    @pl.when(step > 0)
                    def _():
                        z_copy(step - 1, which, *groups[which]).wait_send()

                    if which >= 2:
                        side = which - 2
                        x_copy(step, side).wait_recv()
                        base = 0 if side == 0 else (CX + 1) * tiles
                        for tile in range(tiles):
                            state[now, base + tile, body_rows, :] = x_recv[
                                step, side, tile
                            ].astype(jnp.float32)

            base = (plane + 1) * tiles
            from_left = y_recv[step, group, 0]
            from_right = y_recv[step, group, 1]
            for chunk in range(chunks):
                row = ROWS + chunk * ROWS
                rows = pl.ds(row, ROWS)
                own = pl.ds(chunk * ROWS, ROWS)
                place = plane + chunk * CX
                cells = [state[now, base + tile, rows, :] for tile in range(tiles)]
                up = [pltpu.roll(from_left, lax.rem(LANES - place, LANES), 1)]
                up = up + [pltpu.roll(cell, 1, 1) for cell in cells]
                down = [pltpu.roll(cell, LANES - 1, 1) for cell in cells]
                down = down + [pltpu.roll(from_right, LANES - 1 - place, 1)]
                results = []
                for tile in range(tiles):
                    at = base + tile
                    mine = plane * tiles + tile
                    near = (
                        cells[tile],
                        state[now, at - tiles, rows, :],
                        state[now, at + tiles, rows, :],
                        state[now, at, pl.ds(row - 1, ROWS), :],
                        state[now, at, pl.ds(row + 1, ROWS), :],
                        jnp.where(lane == 0, up[tile], up[tile + 1]),
                        jnp.where(lane == LANES - 1, down[tile + 1], down[tile]),
                    )
                    terms = [weight[k, mine, own, :] * near[k] for k in range(7)]
                    total = ((terms[1] + terms[2]) + (terms[3] + terms[4])) + (
                        (terms[5] + terms[6]) + terms[0]
                    )
                    state[later, at, rows, :] = total
                    results.append(total)

                @pl.when(step < NSTEP - 1)
                def _():
                    pack(step + 1, group, plane, chunk, results[0], results[-1])

            for which in range(4):
                end = starts[which + 1] if which < 3 else CX

                @pl.when(jnp.logical_and(turn == end - 1, step < NSTEP - 1))
                def _():
                    send(step + 1, which)

            @pl.when(step == NSTEP - 1)
            def _():
                for tile in range(tiles):
                    pltpu.make_async_copy(
                        state.at[later, base + tile, body_rows, :],
                        out_ref.at[:, tile_lanes(plane * tiles + tile)],
                        out_sem,
                    ).start()

            return carry

        return lax.fori_loop(0, CX, one, carry)

    lax.fori_loop(0, NSTEP, advance, 0)

    for group in range(4):
        z_copy(NSTEP - 1, group, *groups[group]).wait_send()

    def settle(step, carry):
        for side in range(2):
            x_copy(step, side).wait_send()
            for group in range(4):
                y_copy(step, group, side).wait_send()
        return carry

    lax.fori_loop(0, NSTEP, settle, 0)
    pltpu.make_async_copy(whole, whole, out_sem).wait()


def fast_sweep(theta, courants, coef, waves, n_gx, n_gy, tile_rows):
    levels = theta.shape[0]
    tiles = tile_rows // LANES
    planes = CX * tiles
    slots = (CX + 2) * tiles
    dma = pltpu.SemaphoreType.DMA
    anywhere = pl.BlockSpec(memory_space=pl.ANY)
    return pl.pallas_call(
        functools.partial(sweep_kernel, (n_gx, n_gy, levels, tiles)),
        out_shape=jax.ShapeDtypeStruct(theta.shape, jnp.float32),
        in_specs=[anywhere] * 4,
        out_specs=anywhere,
        scratch_shapes=[
            pltpu.VMEM((2, slots, levels + 2 * ROWS, LANES), jnp.float32),
            pltpu.VMEM((7, planes, levels, LANES), jnp.float32),
            pltpu.VMEM(courants.shape, jnp.bfloat16),
            pltpu.VMEM(coef.shape, jnp.float32),
            pltpu.VMEM(waves.shape, jnp.float32),
            pltpu.VMEM((NSTEP, 2, tiles, levels, LANES), jnp.bfloat16),
            pltpu.VMEM((NSTEP, 2, tiles, levels, LANES), jnp.bfloat16),
            pltpu.VMEM((NSTEP, 4, 2, ROWS, LANES), jnp.float32),
            pltpu.VMEM((NSTEP, 4, 2, ROWS, LANES), jnp.float32),
            dma((4,)),
            dma,
            dma((NSTEP, 2)),
            dma((NSTEP, 2)),
            dma((NSTEP, 4, 2)),
            dma((NSTEP, 4, 2)),
            dma((NSTEP, 4)),
            dma((NSTEP, 4)),
        ],
        compiler_params=pltpu.CompilerParams(
            collective_id=0, has_side_effects=True, vmem_limit_bytes=58 * 1024 * 1024
        ),
        name="transport",
    )(theta, courants, coef, waves)


def body(theta_field, courants, meso_columns, col_weight, owner_ids, line_ids, band_start):
    n_gx, n_gy, n_gz = (lax.axis_size(axis) for axis in ("gx", "gy", "gz"))
    tile_rows = NY // n_gy
    levels = theta_field.shape[2]
    theta_local = theta_field.reshape(levels, CX * tile_rows)
    courant_local = courants.reshape(3, levels, CX * tile_rows)
    column_index = lax.axis_index("gx")
    east_end = column_index == n_gx - 1
    west_end = column_index == 0

    sums = target_spectrum(meso_columns, col_weight, owner_ids, line_ids, band_start, tile_rows)
    sums = lax.psum(sums, ("gx", "gy", "gz"))
    side_sums = jnp.where(east_end, sums[:, 2 * KM :], sums[:, : 2 * KM])
    bands = lax.dynamic_slice_in_dim(band_matrix(), lax.axis_index("gz") * levels, levels, axis=0)
    target = jnp.dot(bands, side_sums, precision=highest, preferred_element_type=jnp.float32)

    own_waves = waves_at(lax.axis_index("gy") * tile_rows + jnp.arange(tile_rows, dtype=jnp.int32))
    width = FW * tile_rows
    strip = jnp.where(east_end, theta_local[:, -width:], theta_local[:, :width])
    strip = strip.reshape(levels, FW, tile_rows).transpose(1, 0, 2)
    spectrum = jnp.einsum(
        "xky,ym->xkm", strip, own_waves, precision=highest, preferred_element_type=jnp.float32
    )
    spectrum = target[None] - lax.psum(spectrum, "gy")
    offsets = jnp.arange(FW, dtype=jnp.float32)
    relaxation = jnp.where(
        east_end, (offsets + 1.0) / FW, jnp.where(west_end, (FW - offsets) / FW, 0.0)
    )
    coef = spectrum * mode_scale()[None, None, :] * relaxation[:, None, None]

    if tile_rows % LANES == 0 and levels == 64 and n_gz == 2 and n_gx > 2 and n_gy > 2:
        result = fast_sweep(
            theta_local, courant_local, coef, own_waves.T, n_gx, n_gy, tile_rows
        )
        return result.reshape(1, 1, levels, CX * tile_rows)

    update = jnp.einsum(
        "xkm,ym->kxy", coef, own_waves, precision=highest, preferred_element_type=jnp.float32
    )
    state_field = theta_local.reshape(levels, CX, tile_rows)
    state_field = jnp.where(
        east_end,
        state_field.at[:, CX - FW :].add(update),
        state_field.at[:, :FW].add(update),
    )
    courant_field = courant_local.reshape(3, levels, CX, tile_rows)
    for step_index in range(NSTEP):
        state_field = sweep_once(state_field, courant_field)
    return state_field.reshape(1, 1, levels, CX * tile_rows)


def solution(mesh):
    in_specs = (
        P("gx", "gy", "gz", None),
        P(None, "gx", "gy", "gz", None),
        P(None, ("gx", "gy", "gz")),
        P(("gx", "gy", "gz")),
        P(("gx", "gy", "gz"), None),
        P(("gx", "gy", "gz")),
        P(("gx", "gy", "gz")),
    )
    out_specs = P("gx", "gy", "gz", None)
    return jax.shard_map(body, mesh=mesh, in_specs=in_specs, out_specs=out_specs, check_vma=False)
```

```python
import functools
import math

import jax
import jax.numpy as jnp
from jax import lax
from jax.experimental import pallas as pl
from jax.experimental.pallas import tpu as pltpu
from jax.sharding import PartitionSpec as P

CX = 16
NY = 3072
ZG = 128
KM = 64
FW = 8
NSTEP = 4
LANES = 128
ROWS = 8

MESH = pl.DeviceIdType.MESH
diffusion = 0.02
highest = lax.Precision.HIGHEST
band_span = 3 * (ZG - 1) // 8 + 2


def extended(array, sides, width, wrap):
    for axis, dim in sides:
        devices, length = (lax.axis_size(axis), array.shape[dim])
        up = [(i, (i + 1) % devices) for i in range(devices if wrap else devices - 1)]
        down = [(j, i) for i, j in up]
        last = lax.slice_in_dim(array, length - width, length, axis=dim)
        initial = lax.slice_in_dim(array, 0, width, axis=dim)
        before = lax.ppermute(last, axis, up)
        after = lax.ppermute(initial, axis, down)
        array = jnp.concatenate([before, array, after], axis=dim)
    return array


def band_matrix():
    levels_z = jnp.arange(ZG, dtype=jnp.int32)
    lower_index = 3 * levels_z // 8
    fraction = (3 * levels_z % 8).astype(jnp.float32) / 8.0
    entries = jnp.arange(band_span, dtype=jnp.int32)[None, :]
    return (1.0 - fraction)[:, None] * (entries == lower_index[:, None]) + fraction[:, None] * (
        entries == lower_index[:, None] + 1
    )


def waves_at(places):
    numbers = jnp.arange(KM, dtype=jnp.int32)
    phases = places[:, None] * numbers[None, :] % NY
    angles = phases.astype(jnp.float32) * (2.0 * math.pi / NY)
    return jnp.concatenate([jnp.cos(angles), jnp.sin(angles)], axis=1)


def mode_scale():
    return jnp.where(jnp.arange(2 * KM, dtype=jnp.int32) % KM == 0, 1.0 / NY, 2.0 / NY).astype(
        jnp.float32
    )


def upwind(state_field, courant_one, ahead_cell, behind_cell):
    return -jnp.maximum(courant_one, 0.0) * (state_field - behind_cell) - jnp.minimum(
        courant_one, 0.0
    ) * (ahead_cell - state_field)


def sweep_once(state_field, courant_local):
    side_cells = extended(state_field, (("gx", 1), ("gy", 2)), 1, True)
    level_cells = extended(state_field, (("gz", 0),), 1, False)
    pairs = (
        (side_cells[:, 2:, 1:-1], side_cells[:, :-2, 1:-1]),
        (level_cells[2:], level_cells[:-2]),
        (side_cells[:, 1:-1, 2:], side_cells[:, 1:-1, :-2]),
    )
    change = 0.0
    neighbours = 0.0
    for direction, (ahead, behind) in enumerate(pairs):
        change = change + upwind(
            state_field, courant_local[direction].astype(jnp.float32), ahead, behind
        )
        neighbours = neighbours + ahead + behind
    return state_field + change + diffusion * (neighbours - 6.0 * state_field)


def target_spectrum(meso_columns, col_weight, owner_ids, line_ids, band_start, tile_rows):
    owners = owner_ids[:, 0]
    places = owners // 2 * tile_rows + line_ids
    waves = waves_at(places) * col_weight[:, None]
    sided = jnp.concatenate(
        [jnp.where((owners % 2 == side)[:, None], waves, 0.0) for side in range(2)], axis=1
    )
    shifted = jnp.zeros((band_span, meso_columns.shape[1]), jnp.float32)
    for offset in range(meso_columns.shape[0] - band_span + 1):
        shifted = shifted + jnp.where(
            band_start[None, :] == offset, meso_columns[offset : offset + band_span], 0.0
        )
    return jnp.dot(shifted, sided, precision=highest, preferred_element_type=jnp.float32)


def sweep_kernel(
    sizes,
    theta_ref,
    courant_ref,
    coef_ref,
    waves_ref,
    out_ref,
    state_a,
    state_b,
    weight,
    courant,
    coef,
    waves,
    x_send,
    x_recv,
    y_send,
    y_recv,
    in_sem,
    out_sem,
    xs_sem,
    xr_sem,
    ys_sem,
    yr_sem,
    zs_sem,
    zr_sem,
):
    n_gx, n_gy, levels, tiles = sizes
    chunks = levels // ROWS
    planes = CX * tiles
    gx, gy, gz = (lax.axis_index(axis) for axis in ("gx", "gy", "gz"))
    x_right, x_left = lax.rem(gx + 1, n_gx), lax.rem(gx + n_gx - 1, n_gx)
    y_right, y_left = lax.rem(gy + 1, n_gy), lax.rem(gy + n_gy - 1, n_gy)
    other = 1 - gz
    east_end = gx == n_gx - 1
    west_end = gx == 0
    body_rows = pl.ds(ROWS, levels)

    def tile_lanes(tile):
        return pl.ds(pl.multiple_of(tile * LANES, LANES), LANES)

    courant_copy = pltpu.make_async_copy(courant_ref, courant, in_sem.at[1])
    coef_copy = pltpu.make_async_copy(coef_ref, coef, in_sem.at[2])
    waves_copy = pltpu.make_async_copy(waves_ref, waves, in_sem.at[3])

    def fetch(tile, carry):
        pltpu.make_async_copy(
            theta_ref.at[:, tile_lanes(tile)],
            state_a.at[tile + tiles, body_rows, :],
            in_sem.at[0],
        ).start()
        return carry

    courant_copy.start()
    lax.fori_loop(0, planes, fetch, 0)
    coef_copy.start()
    waves_copy.start()

    barrier = pltpu.get_barrier_semaphore()
    neighbours = (
        {"gx": x_right},
        {"gx": x_left},
        {"gy": y_right},
        {"gy": y_left},
        {"gz": other},
    )
    for neighbour in neighbours:
        pl.semaphore_signal(barrier, inc=1, device_id=neighbour, device_id_type=MESH)

    zero_rows = pl.ds(pl.multiple_of(jnp.where(gz == 0, 0, ROWS + levels), ROWS), ROWS)

    def blank(tile, carry):
        for state in (state_a, state_b):
            state[tile + tiles, zero_rows, :] = jnp.zeros((ROWS, LANES), jnp.float32)
        return carry

    lax.fori_loop(0, planes, blank, 0)
    y_send[...] = jnp.zeros_like(y_send)
    lane = lax.broadcasted_iota(jnp.int32, (ROWS, LANES), 1)

    courant_copy.wait()

    def weigh(tile, carry):
        centre = 1.0
        for direction in range(3):
            number = courant[direction, :, tile_lanes(tile)].astype(jnp.float32)
            upward = jnp.maximum(number, 0.0)
            behind = upward + diffusion
            ahead = (upward - number) + diffusion
            weight[2 * direction + 1, tile] = behind
            weight[2 * direction + 2, tile] = ahead
            centre = centre - (behind + ahead)
        weight[0, tile] = centre
        return carry

    lax.fori_loop(0, planes, weigh, 0)

    whole = state_a.at[pl.ds(tiles, planes), body_rows, :]
    pltpu.make_async_copy(whole, whole, in_sem.at[0]).wait()
    coef_copy.wait()
    waves_copy.wait()

    @pl.when(jnp.logical_or(west_end, east_end))
    def _():
        first = jnp.where(east_end, CX - FW, 0)

        def nudge(index, carry):
            smooth = jnp.dot(
                coef[index], waves[...], precision=highest, preferred_element_type=jnp.float32
            )
            base = (first + index + 1) * tiles
            for tile in range(tiles):
                state_a[base + tile, body_rows, :] += smooth[:, tile * LANES : (tile + 1) * LANES]
            return carry

        lax.fori_loop(0, FW, nudge, 0)

    source_rows = pl.ds(pl.multiple_of(jnp.where(gz == 0, levels, ROWS), ROWS), ROWS)
    target_rows = pl.ds(pl.multiple_of(jnp.where(gz == 0, 0, ROWS + levels), ROWS), ROWS)

    def z_copy(state, step, group):
        first, count = groups[group]
        some = pl.ds((first + 1) * tiles, count * tiles)
        return pltpu.make_async_remote_copy(
            src_ref=state.at[some, source_rows, :],
            dst_ref=state.at[some, target_rows, :],
            send_sem=zs_sem.at[step, group],
            recv_sem=zr_sem.at[step, group],
            device_id={"gz": other},
            device_id_type=MESH,
        )

    def y_copy(step, group, side):
        return pltpu.make_async_remote_copy(
            src_ref=y_send.at[step, group, side],
            dst_ref=y_recv.at[step, group, side],
            send_sem=ys_sem.at[step, group, side],
            recv_sem=yr_sem.at[step, group, side],
            device_id={"gy": y_right if side == 0 else y_left},
            device_id_type=MESH,
        )

    def x_copy(step, side):
        return pltpu.make_async_remote_copy(
            src_ref=x_send.at[step, side],
            dst_ref=x_recv.at[step, side],
            send_sem=xs_sem.at[step, side],
            recv_sem=xr_sem.at[step, side],
            device_id={"gx": x_right if side == 0 else x_left},
            device_id_type=MESH,
        )

    half = (CX - 2) // 2
    groups = ((1, half), (1 + half, half), (0, 1), (CX - 1, 1))

    def pack(step, group, plane, edges):
        right, left = y_send[step, group, 0], y_send[step, group, 1]
        for chunk, (low, high) in enumerate(edges):
            place = plane + chunk * CX
            here = lane == place
            right = jnp.where(here, pltpu.roll(high, lax.rem(place + 1, LANES), 1), right)
            left = jnp.where(here, pltpu.roll(low, place, 1), left)
        y_send[step, group, 0] = right
        y_send[step, group, 1] = left

    def send(state, step, group):
        z_copy(state, step, group).start()
        for side in range(2):
            y_copy(step, group, side).start()
        if group >= 2:
            side = 3 - group
            base = (groups[group][0] + 1) * tiles
            for tile in range(tiles):
                x_send[step, side, tile] = state[base + tile, body_rows, :].astype(jnp.bfloat16)
            x_copy(step, side).start()

    pl.semaphore_wait(barrier, len(neighbours))

    def plane_of(turn):
        plane = jnp.where(turn < 2 * half, turn + 1, jnp.where(turn == 2 * half, 0, CX - 1))
        group = jnp.where(
            turn < half, 0, jnp.where(turn < 2 * half, 1, jnp.where(turn == 2 * half, 2, 3))
        )
        return plane, group

    def pack_start(turn, carry):
        plane, group = plane_of(turn)
        base = (plane + 1) * tiles
        edges = []
        for chunk in range(chunks):
            rows = pl.ds(ROWS + chunk * ROWS, ROWS)
            edges.append((state_a[base, rows, :], state_a[base + tiles - 1, rows, :]))
        pack(0, group, plane, edges)
        return carry

    lax.fori_loop(0, CX, pack_start, 0)
    for group in (2, 3, 0, 1):
        send(state_a, 0, group)

    starts = (0, half, 2 * half, 2 * half + 1)

    def advance(step, now, later, final):
        def one(turn, carry):
            plane, group = plane_of(turn)
            for which in range(4):

                @pl.when(turn == starts[which])
                def _():
                    z_copy(now, step, which).wait_recv()
                    for side in range(2):
                        y_copy(step, which, side).wait_recv()

                    @pl.when(step > 0)
                    def _():
                        z_copy(later, step - 1, which).wait_send()

                    if which >= 2:
                        side = which - 2
                        x_copy(step, side).wait_recv()
                        base = 0 if side == 0 else (CX + 1) * tiles
                        for tile in range(tiles):
                            now[base + tile, body_rows, :] = x_recv[step, side, tile].astype(
                                jnp.float32
                            )

            base = (plane + 1) * tiles
            from_left = y_recv[step, group, 0]
            from_right = y_recv[step, group, 1]
            edges = []
            for chunk in range(chunks):
                row = ROWS + chunk * ROWS
                rows = pl.ds(row, ROWS)
                own = pl.ds(chunk * ROWS, ROWS)
                place = plane + chunk * CX
                cells = [now[base + tile, rows, :] for tile in range(tiles)]
                up = [pltpu.roll(from_left, lax.rem(LANES - place, LANES), 1)]
                up = up + [pltpu.roll(cell, 1, 1) for cell in cells]
                down = [pltpu.roll(cell, LANES - 1, 1) for cell in cells]
                down = down + [pltpu.roll(from_right, LANES - 1 - place, 1)]
                results = []
                for tile in range(tiles):
                    at = base + tile
                    mine = plane * tiles + tile
                    near = (
                        cells[tile],
                        now[at - tiles, rows, :],
                        now[at + tiles, rows, :],
                        now[at, pl.ds(row - 1, ROWS), :],
                        now[at, pl.ds(row + 1, ROWS), :],
                        jnp.where(lane == 0, up[tile], up[tile + 1]),
                        jnp.where(lane == LANES - 1, down[tile + 1], down[tile]),
                    )
                    terms = [weight[k, mine, own, :] * near[k] for k in range(7)]
                    total = ((terms[1] + terms[2]) + (terms[3] + terms[4])) + (
                        (terms[5] + terms[6]) + terms[0]
                    )
                    later[at, rows, :] = total
                    results.append(total)
                edges.append((results[0], results[-1]))
            pack(step + 1, group, plane, edges)

            for which in range(4):
                end = starts[which + 1] if which < 3 else CX

                @pl.when(jnp.logical_and(turn == end - 1, step < NSTEP - 1))
                def _():
                    send(later, step + 1, which)

            if final:

                @pl.when(step == NSTEP - 1)
                def _():
                    for tile in range(tiles):
                        pltpu.make_async_copy(
                            later.at[base + tile, body_rows, :],
                            out_ref.at[:, tile_lanes(plane * tiles + tile)],
                            out_sem,
                        ).start()

            return carry

        lax.fori_loop(0, CX, one, 0)

    def two(pair, carry):
        advance(2 * pair, state_a, state_b, False)
        advance(2 * pair + 1, state_b, state_a, True)
        return carry

    lax.fori_loop(0, NSTEP // 2, two, 0)

    for group in range(4):
        z_copy(state_b, NSTEP - 1, group).wait_send()

    def settle(step, carry):
        for side in range(2):
            x_copy(step, side).wait_send()
            for group in range(4):
                y_copy(step, group, side).wait_send()
        return carry

    lax.fori_loop(0, NSTEP, settle, 0)
    pltpu.make_async_copy(whole, whole, out_sem).wait()


def fast_sweep(theta, courants, coef, waves, n_gx, n_gy, tile_rows):
    levels = theta.shape[0]
    tiles = tile_rows // LANES
    planes = CX * tiles
    slots = (CX + 2) * tiles
    dma = pltpu.SemaphoreType.DMA
    anywhere = pl.BlockSpec(memory_space=pl.ANY)
    return pl.pallas_call(
        functools.partial(sweep_kernel, (n_gx, n_gy, levels, tiles)),
        out_shape=jax.ShapeDtypeStruct(theta.shape, jnp.float32),
        in_specs=[anywhere] * 4,
        out_specs=anywhere,
        scratch_shapes=[
            pltpu.VMEM((slots, levels + 2 * ROWS, LANES), jnp.float32),
            pltpu.VMEM((slots, levels + 2 * ROWS, LANES), jnp.float32),
            pltpu.VMEM((7, planes, levels, LANES), jnp.float32),
            pltpu.VMEM(courants.shape, jnp.bfloat16),
            pltpu.VMEM(coef.shape, jnp.float32),
            pltpu.VMEM(waves.shape, jnp.float32),
            pltpu.VMEM((NSTEP, 2, tiles, levels, LANES), jnp.bfloat16),
            pltpu.VMEM((NSTEP, 2, tiles, levels, LANES), jnp.bfloat16),
            pltpu.VMEM((NSTEP + 1, 4, 2, ROWS, LANES), jnp.float32),
            pltpu.VMEM((NSTEP, 4, 2, ROWS, LANES), jnp.float32),
            dma((4,)),
            dma,
            dma((NSTEP, 2)),
            dma((NSTEP, 2)),
            dma((NSTEP, 4, 2)),
            dma((NSTEP, 4, 2)),
            dma((NSTEP, 4)),
            dma((NSTEP, 4)),
        ],
        compiler_params=pltpu.CompilerParams(
            collective_id=0, has_side_effects=True, vmem_limit_bytes=58 * 1024 * 1024
        ),
        name="transport",
    )(theta, courants, coef, waves)


def body(theta_field, courants, meso_columns, col_weight, owner_ids, line_ids, band_start):
    n_gx, n_gy, n_gz = (lax.axis_size(axis) for axis in ("gx", "gy", "gz"))
    tile_rows = NY // n_gy
    levels = theta_field.shape[2]
    theta_local = theta_field.reshape(levels, CX * tile_rows)
    courant_local = courants.reshape(3, levels, CX * tile_rows)
    column_index = lax.axis_index("gx")
    east_end = column_index == n_gx - 1
    west_end = column_index == 0

    sums = target_spectrum(meso_columns, col_weight, owner_ids, line_ids, band_start, tile_rows)
    sums = lax.psum(sums, ("gx", "gy", "gz"))
    side_sums = jnp.where(east_end, sums[:, 2 * KM :], sums[:, : 2 * KM])
    bands = lax.dynamic_slice_in_dim(band_matrix(), lax.axis_index("gz") * levels, levels, axis=0)
    target = jnp.dot(bands, side_sums, precision=highest, preferred_element_type=jnp.float32)

    own_waves = waves_at(lax.axis_index("gy") * tile_rows + jnp.arange(tile_rows, dtype=jnp.int32))
    width = FW * tile_rows
    strip = jnp.where(east_end, theta_local[:, -width:], theta_local[:, :width])
    strip = strip.reshape(levels, FW, tile_rows).transpose(1, 0, 2)
    spectrum = jnp.einsum(
        "xky,ym->xkm", strip, own_waves, precision=highest, preferred_element_type=jnp.float32
    )
    spectrum = target[None] - lax.psum(spectrum, "gy")
    offsets = jnp.arange(FW, dtype=jnp.float32)
    relaxation = jnp.where(
        east_end, (offsets + 1.0) / FW, jnp.where(west_end, (FW - offsets) / FW, 0.0)
    )
    coef = spectrum * mode_scale()[None, None, :] * relaxation[:, None, None]

    if tile_rows % LANES == 0 and levels == 64 and n_gz == 2 and n_gx > 2 and n_gy > 2:
        result = fast_sweep(
            theta_local, courant_local, coef, own_waves.T, n_gx, n_gy, tile_rows
        )
        return result.reshape(1, 1, levels, CX * tile_rows)

    update = jnp.einsum(
        "xkm,ym->kxy", coef, own_waves, precision=highest, preferred_element_type=jnp.float32
    )
    state_field = theta_local.reshape(levels, CX, tile_rows)
    state_field = jnp.where(
        east_end,
        state_field.at[:, CX - FW :].add(update),
        state_field.at[:, :FW].add(update),
    )
    courant_field = courant_local.reshape(3, levels, CX, tile_rows)
    for step_index in range(NSTEP):
        state_field = sweep_once(state_field, courant_field)
    return state_field.reshape(1, 1, levels, CX * tile_rows)


def solution(mesh):
    in_specs = (
        P("gx", "gy", "gz", None),
        P(None, "gx", "gy", "gz", None),
        P(None, ("gx", "gy", "gz")),
        P(("gx", "gy", "gz")),
        P(("gx", "gy", "gz"), None),
        P(("gx", "gy", "gz")),
        P(("gx", "gy", "gz")),
    )
    out_specs = P("gx", "gy", "gz", None)
    return jax.shard_map(body, mesh=mesh, in_specs=in_specs, out_specs=out_specs, check_vma=False)
```

```python
import functools
import math

import jax
import jax.numpy as jnp
from jax import lax
from jax.experimental import pallas as pl
from jax.experimental.pallas import tpu as pltpu
from jax.sharding import PartitionSpec as P

CX = 16
NY = 3072
ZG = 128
KM = 64
FW = 8
NSTEP = 4
LANES = 128
ROWS = 8

MESH = pl.DeviceIdType.MESH
diffusion = 0.02
highest = lax.Precision.HIGHEST
band_span = 3 * (ZG - 1) // 8 + 2
ENTRIES = 64
BAND_STEP = 24
BAND_ROWS = 32


def extended(array, sides, width, wrap):
    for axis, dim in sides:
        devices, length = (lax.axis_size(axis), array.shape[dim])
        up = [(i, (i + 1) % devices) for i in range(devices if wrap else devices - 1)]
        down = [(j, i) for i, j in up]
        last = lax.slice_in_dim(array, length - width, length, axis=dim)
        initial = lax.slice_in_dim(array, 0, width, axis=dim)
        before = lax.ppermute(last, axis, up)
        after = lax.ppermute(initial, axis, down)
        array = jnp.concatenate([before, array, after], axis=dim)
    return array


def band_matrix():
    levels_z = jnp.arange(ZG, dtype=jnp.int32)
    lower_index = 3 * levels_z // 8
    fraction = (3 * levels_z % 8).astype(jnp.float32) / 8.0
    entries = jnp.arange(band_span, dtype=jnp.int32)[None, :]
    return (1.0 - fraction)[:, None] * (entries == lower_index[:, None]) + fraction[:, None] * (
        entries == lower_index[:, None] + 1
    )


def waves_at(places):
    numbers = jnp.arange(KM, dtype=jnp.int32)
    phases = places[:, None] * numbers[None, :] % NY
    angles = phases.astype(jnp.float32) * (2.0 * math.pi / NY)
    return jnp.concatenate([jnp.cos(angles), jnp.sin(angles)], axis=1)


def mode_scale():
    return jnp.where(jnp.arange(2 * KM, dtype=jnp.int32) % KM == 0, 1.0 / NY, 2.0 / NY).astype(
        jnp.float32
    )


def upwind(state_field, courant_one, ahead_cell, behind_cell):
    return -jnp.maximum(courant_one, 0.0) * (state_field - behind_cell) - jnp.minimum(
        courant_one, 0.0
    ) * (ahead_cell - state_field)


def sweep_once(state_field, courant_local):
    side_cells = extended(state_field, (("gx", 1), ("gy", 2)), 1, True)
    level_cells = extended(state_field, (("gz", 0),), 1, False)
    pairs = (
        (side_cells[:, 2:, 1:-1], side_cells[:, :-2, 1:-1]),
        (level_cells[2:], level_cells[:-2]),
        (side_cells[:, 1:-1, 2:], side_cells[:, 1:-1, :-2]),
    )
    change = 0.0
    neighbours = 0.0
    for direction, (ahead, behind) in enumerate(pairs):
        change = change + upwind(
            state_field, courant_local[direction].astype(jnp.float32), ahead, behind
        )
        neighbours = neighbours + ahead + behind
    return state_field + change + diffusion * (neighbours - 6.0 * state_field)


def target_spectrum(meso_columns, col_weight, owner_ids, line_ids, band_start, tile_rows):
    owners = owner_ids[:, 0]
    places = owners // 2 * tile_rows + line_ids
    waves = waves_at(places) * col_weight[:, None]
    sided = jnp.concatenate(
        [jnp.where((owners % 2 == side)[:, None], waves, 0.0) for side in range(2)], axis=1
    )
    shifted = jnp.zeros((band_span, meso_columns.shape[1]), jnp.float32)
    for offset in range(meso_columns.shape[0] - band_span + 1):
        shifted = shifted + jnp.where(
            band_start[None, :] == offset, meso_columns[offset : offset + band_span], 0.0
        )
    return jnp.dot(shifted, sided, precision=highest, preferred_element_type=jnp.float32)


def waves_of(places):
    numbers = lax.broadcasted_iota(jnp.int32, (KM, places.shape[1]), 0).astype(jnp.float32)
    turns = numbers * places
    quarter = NY // 4
    quarters = jnp.floor(turns * (1.0 / quarter) + 0.5)
    angle = (turns - quarter * quarters) * (2.0 * math.pi / NY)
    square = angle * angle
    sine = 1.0 / 362880.0
    for factor in (-1.0 / 5040.0, 1.0 / 120.0, -1.0 / 6.0, 1.0):
        sine = sine * square + factor
    sine = sine * angle
    cosine = 1.0 / 40320.0
    for factor in (-1.0 / 720.0, 1.0 / 24.0, -0.5, 1.0):
        cosine = cosine * square + factor
    corner = quarters - 4.0 * jnp.floor(quarters * 0.25)
    odd = jnp.logical_or(corner == 1.0, corner == 3.0)
    cos_values = jnp.where(odd, sine, cosine)
    sin_values = jnp.where(odd, cosine, sine)
    cos_values = jnp.where(
        jnp.logical_or(corner == 1.0, corner == 2.0), -cos_values, cos_values
    )
    sin_values = jnp.where(corner >= 2.0, -sin_values, sin_values)
    return jnp.concatenate([cos_values, sin_values], axis=0)


def dot_rows(left, right):
    return lax.dot_general(
        left,
        right,
        (((1,), (1,)), ((), ())),
        precision=highest,
        preferred_element_type=jnp.float32,
    )


def sweep_kernel(
    sizes,
    theta_ref,
    courant_ref,
    meso_ref,
    col_weight_ref,
    codes_ref,
    out_ref,
    state_a,
    state_b,
    weight,
    courant,
    meso,
    col_weight,
    codes,
    waves,
    sum_send,
    sum_recv,
    part,
    part_recv,
    coef,
    x_send,
    x_recv,
    y_send,
    y_recv,
    in_sem,
    out_sem,
    xs_sem,
    xr_sem,
    ys_sem,
    yr_sem,
    zs_sem,
    zr_sem,
    ss_sem,
    sr_sem,
    ps_sem,
    pr_sem,
    cs_sem,
    cr_sem,
):
    n_gx, n_gy, levels, tiles = sizes
    chunks = levels // ROWS
    planes = CX * tiles
    gx, gy, gz = (lax.axis_index(axis) for axis in ("gx", "gy", "gz"))
    x_right, x_left = lax.rem(gx + 1, n_gx), lax.rem(gx + n_gx - 1, n_gx)
    y_right, y_left = lax.rem(gy + 1, n_gy), lax.rem(gy + n_gy - 1, n_gy)
    other = 1 - gz
    east_end = gx == n_gx - 1
    west_end = gx == 0
    body_rows = pl.ds(ROWS, levels)

    def tile_lanes(tile):
        return pl.ds(pl.multiple_of(tile * LANES, LANES), LANES)

    courant_copy = pltpu.make_async_copy(courant_ref, courant, in_sem.at[1])
    column_copies = [
        pltpu.make_async_copy(meso_ref, meso, in_sem.at[2]),
        pltpu.make_async_copy(col_weight_ref, col_weight, in_sem.at[3]),
        pltpu.make_async_copy(codes_ref, codes, in_sem.at[4]),
    ]

    def fetch(tile, carry):
        pltpu.make_async_copy(
            theta_ref.at[:, tile_lanes(tile)],
            state_a.at[tile + tiles, body_rows, :],
            in_sem.at[0],
        ).start()
        return carry

    for copy in column_copies:
        copy.start()
    lax.fori_loop(0, planes, fetch, 0)
    courant_copy.start()

    barrier = pltpu.get_barrier_semaphore()
    greeted = 0
    for step_x in range(n_gx):
        for step_z in range(2):
            if step_x + step_z > 0:
                friend = {"gx": lax.rem(gx + step_x, n_gx), "gz": lax.rem(gz + step_z, 2)}
                pl.semaphore_signal(barrier, inc=1, device_id=friend, device_id_type=MESH)
                greeted += 1
    for step_y in range(1, n_gy):
        friend = {"gy": lax.rem(gy + step_y, n_gy)}
        pl.semaphore_signal(barrier, inc=1, device_id=friend, device_id_type=MESH)
        greeted += 1

    tile_rows = tiles * LANES
    row_places = lax.broadcasted_iota(jnp.int32, (1, tile_rows), 1) + gy * tile_rows
    waves[...] = waves_of(row_places.astype(jnp.float32))
    for copy in column_copies:
        copy.wait()
    owners, lines, bands = codes[0:1, :], codes[1:2, :], codes[2:3, :]
    column_count = meso.shape[1]
    places = jnp.right_shift(owners, 1) * tile_rows + lines
    column_waves = waves_of(places.astype(jnp.float32))
    entries = meso.shape[0]
    shifted = jnp.concatenate(
        [meso[...], jnp.zeros((ENTRIES - entries, column_count), jnp.float32)], axis=0
    )
    for bit in range(4):
        moved = pltpu.roll(shifted, ENTRIES - (1 << bit), 0)
        chosen = jnp.bitwise_and(jnp.right_shift(bands, bit), 1) == 1
        shifted = jnp.where(chosen, moved, shifted)
    for side in range(2):
        side_weight = jnp.where(jnp.bitwise_and(owners, 1) == side, col_weight[...], 0.0)
        sum_send[side] = dot_rows(shifted * side_weight, column_waves)

    pl.semaphore_wait(barrier, greeted)

    def sum_copy(side, half_z):
        return pltpu.make_async_remote_copy(
            src_ref=sum_send.at[side, pl.ds(BAND_STEP * half_z, BAND_ROWS), :],
            dst_ref=sum_recv.at[2 * gx + gz],
            send_sem=ss_sem.at[side, half_z],
            recv_sem=sr_sem.at[2 * gx + gz],
            device_id={"gx": side * (n_gx - 1), "gz": half_z},
            device_id_type=MESH,
        )

    def each_sum(act, act_here):
        for side in range(2):
            for half_z in range(2):
                here = jnp.logical_and(gx == side * (n_gx - 1), gz == half_z)

                @pl.when(jnp.logical_not(here))
                def _():
                    act(sum_copy(side, half_z))

                if act_here is not None:

                    @pl.when(here)
                    def _():
                        act_here(side, half_z)

    def keep_sum(side, half_z):
        start = BAND_STEP * half_z
        sum_recv[2 * gx + gz] = sum_send[side, start : start + BAND_ROWS, :]

    each_sum(lambda copy: copy.start(), keep_sum)

    zero_rows = pl.ds(pl.multiple_of(jnp.where(gz == 0, 0, ROWS + levels), ROWS), ROWS)

    def blank(tile, carry):
        for state in (state_a, state_b):
            state[tile + tiles, zero_rows, :] = jnp.zeros((ROWS, LANES), jnp.float32)
        return carry

    lax.fori_loop(0, planes, blank, 0)
    y_send[...] = jnp.zeros_like(y_send)
    lane = lax.broadcasted_iota(jnp.int32, (ROWS, LANES), 1)

    whole = state_a.at[pl.ds(tiles, planes), body_rows, :]
    pltpu.make_async_copy(whole, whole, in_sem.at[0]).wait()

    fringe = jnp.logical_or(west_end, east_end)
    first = jnp.where(east_end, CX - FW, 0)
    share = FW // n_gy

    def part_copy(peer):
        return pltpu.make_async_remote_copy(
            src_ref=part.at[pl.ds(peer * share, share)],
            dst_ref=part_recv.at[gy],
            send_sem=ps_sem.at[peer],
            recv_sem=pr_sem.at[gy],
            device_id={"gy": peer},
            device_id_type=MESH,
        )

    def part_arrival(peer):
        return pltpu.make_async_remote_copy(
            src_ref=part.at[pl.ds(peer * share, share)],
            dst_ref=part_recv.at[peer],
            send_sem=ps_sem.at[peer],
            recv_sem=pr_sem.at[peer],
            device_id={"gy": peer},
            device_id_type=MESH,
        )

    def coef_copy(peer, owner):
        return pltpu.make_async_remote_copy(
            src_ref=coef.at[pl.ds(owner * share, share)],
            dst_ref=coef.at[pl.ds(owner * share, share)],
            send_sem=cs_sem.at[peer],
            recv_sem=cr_sem.at[owner],
            device_id={"gy": peer},
            device_id_type=MESH,
        )

    peers = [lax.rem(gy + step_y, n_gy) for step_y in range(1, n_gy)]

    @pl.when(fringe)
    def _():
        def strip_spectrum(index, carry):
            base = (first + index + 1) * tiles
            strip = jnp.concatenate(
                [state_a[base + tile, body_rows, :] for tile in range(tiles)], axis=1
            )
            part[index] = dot_rows(strip, waves[...])
            return carry

        lax.fori_loop(0, FW, strip_spectrum, 0)

        total = jnp.zeros((BAND_ROWS, 2 * KM), jnp.float32)
        for slot in range(2 * n_gx):

            @pl.when(slot != 2 * gx + gz)
            def _():
                pltpu.make_async_remote_copy(
                    src_ref=sum_send.at[0, pl.ds(0, BAND_ROWS), :],
                    dst_ref=sum_recv.at[slot],
                    send_sem=ss_sem.at[0, 0],
                    recv_sem=sr_sem.at[slot],
                    device_id={"gz": other},
                    device_id_type=MESH,
                ).wait_recv()

        for slot in range(2 * n_gx):
            total = total + sum_recv[slot]
        level = lax.broadcasted_iota(jnp.int32, (levels, BAND_ROWS), 0) + gz * levels
        entry = lax.broadcasted_iota(jnp.int32, (levels, BAND_ROWS), 1) + gz * BAND_STEP
        lower = jnp.right_shift(3 * level, 3)
        fraction = jnp.bitwise_and(3 * level, 7).astype(jnp.float32) * 0.125
        band = jnp.where(entry == lower, 1.0 - fraction, 0.0) + jnp.where(
            entry == lower + 1, fraction, 0.0
        )
        target = jnp.dot(band, total, precision=highest, preferred_element_type=jnp.float32)

        def subtract(index, carry):
            part[index] = target - part[index]
            return carry

        lax.fori_loop(0, FW, subtract, 0)
        for peer in peers:
            part_copy(peer).start()

    courant_copy.wait()

    def weigh(tile, carry):
        centre = 1.0
        for direction in range(3):
            number = courant[direction, :, tile_lanes(tile)].astype(jnp.float32)
            upward = jnp.maximum(number, 0.0)
            behind = upward + diffusion
            ahead = (upward - number) + diffusion
            weight[2 * direction + 1, tile] = behind
            weight[2 * direction + 2, tile] = ahead
            centre = centre - (behind + ahead)
        weight[0, tile] = centre
        return carry

    lax.fori_loop(0, planes, weigh, 0)

    @pl.when(fringe)
    def _():
        for peer in peers:
            part_arrival(peer).wait_recv()
        mode = lax.broadcasted_iota(jnp.int32, (levels, 2 * KM), 1)
        scale = jnp.where(jnp.bitwise_and(mode, KM - 1) == 0, 1.0 / NY, 2.0 / NY)
        for index in range(share):
            plane = gy * share + index
            total = part[plane]
            for peer in peers:
                total = total + part_recv[peer, index]
            steps = jnp.where(east_end, plane + 1, FW - plane).astype(jnp.float32)
            coef[plane] = (total * (scale * (steps * (1.0 / FW)))).astype(jnp.bfloat16)
        for peer in peers:
            coef_copy(peer, gy).start()
        for peer in peers:
            coef_copy(peer, peer).wait_recv()

        def nudge(index, carry):
            smooth = jnp.dot(
                coef[index].astype(jnp.float32),
                waves[...],
                precision=highest,
                preferred_element_type=jnp.float32,
            )
            base = (first + index + 1) * tiles
            for tile in range(tiles):
                state_a[base + tile, body_rows, :] += smooth[:, tile * LANES : (tile + 1) * LANES]
            return carry

        lax.fori_loop(0, FW, nudge, 0)

    source_rows = pl.ds(pl.multiple_of(jnp.where(gz == 0, levels, ROWS), ROWS), ROWS)
    target_rows = pl.ds(pl.multiple_of(jnp.where(gz == 0, 0, ROWS + levels), ROWS), ROWS)

    def z_copy(state, step, group):
        first, count = groups[group]
        some = pl.ds((first + 1) * tiles, count * tiles)
        return pltpu.make_async_remote_copy(
            src_ref=state.at[some, source_rows, :],
            dst_ref=state.at[some, target_rows, :],
            send_sem=zs_sem.at[step, group],
            recv_sem=zr_sem.at[step, group],
            device_id={"gz": other},
            device_id_type=MESH,
        )

    def y_copy(step, group, side):
        return pltpu.make_async_remote_copy(
            src_ref=y_send.at[step, group, side],
            dst_ref=y_recv.at[step, group, side],
            send_sem=ys_sem.at[step, group, side],
            recv_sem=yr_sem.at[step, group, side],
            device_id={"gy": y_right if side == 0 else y_left},
            device_id_type=MESH,
        )

    def x_copy(step, side):
        return pltpu.make_async_remote_copy(
            src_ref=x_send.at[step, side],
            dst_ref=x_recv.at[step, side],
            send_sem=xs_sem.at[step, side],
            recv_sem=xr_sem.at[step, side],
            device_id={"gx": x_right if side == 0 else x_left},
            device_id_type=MESH,
        )

    half = (CX - 2) // 2
    groups = ((1, half), (1 + half, half), (0, 1), (CX - 1, 1))

    def pack(step, group, plane, edges):
        right, left = y_send[step, group, 0], y_send[step, group, 1]
        for chunk, (low, high) in enumerate(edges):
            place = plane + chunk * CX
            here = lane == place
            right = jnp.where(here, pltpu.roll(high, lax.rem(place + 1, LANES), 1), right)
            left = jnp.where(here, pltpu.roll(low, place, 1), left)
        y_send[step, group, 0] = right
        y_send[step, group, 1] = left

    def send(state, step, group):
        z_copy(state, step, group).start()
        for side in range(2):
            y_copy(step, group, side).start()
        if group >= 2:
            side = 3 - group
            base = (groups[group][0] + 1) * tiles
            for tile in range(tiles):
                x_send[step, side, tile] = state[base + tile, body_rows, :].astype(jnp.bfloat16)
            x_copy(step, side).start()

    def plane_of(turn):
        plane = jnp.where(turn < 2 * half, turn + 1, jnp.where(turn == 2 * half, 0, CX - 1))
        group = jnp.where(
            turn < half, 0, jnp.where(turn < 2 * half, 1, jnp.where(turn == 2 * half, 2, 3))
        )
        return plane, group

    def pack_start(turn, carry):
        plane, group = plane_of(turn)
        base = (plane + 1) * tiles
        edges = []
        for chunk in range(chunks):
            rows = pl.ds(ROWS + chunk * ROWS, ROWS)
            edges.append((state_a[base, rows, :], state_a[base + tiles - 1, rows, :]))
        pack(0, group, plane, edges)
        return carry

    lax.fori_loop(0, CX, pack_start, 0)
    for group in (2, 3, 0, 1):
        send(state_a, 0, group)

    starts = (0, half, 2 * half, 2 * half + 1)

    def advance(step, now, later, final):
        def one(turn, carry):
            plane, group = plane_of(turn)
            for which in range(4):

                @pl.when(turn == starts[which])
                def _():
                    z_copy(now, step, which).wait_recv()
                    for side in range(2):
                        y_copy(step, which, side).wait_recv()

                    @pl.when(step > 0)
                    def _():
                        z_copy(later, step - 1, which).wait_send()

                    if which >= 2:
                        side = which - 2
                        x_copy(step, side).wait_recv()
                        base = 0 if side == 0 else (CX + 1) * tiles
                        for tile in range(tiles):
                            now[base + tile, body_rows, :] = x_recv[step, side, tile].astype(
                                jnp.float32
                            )

            base = (plane + 1) * tiles
            from_left = y_recv[step, group, 0]
            from_right = y_recv[step, group, 1]
            edges = []
            for chunk in range(chunks):
                row = ROWS + chunk * ROWS
                rows = pl.ds(row, ROWS)
                own = pl.ds(chunk * ROWS, ROWS)
                place = plane + chunk * CX
                cells = [now[base + tile, rows, :] for tile in range(tiles)]
                up = [pltpu.roll(from_left, lax.rem(LANES - place, LANES), 1)]
                up = up + [pltpu.roll(cell, 1, 1) for cell in cells]
                down = [pltpu.roll(cell, LANES - 1, 1) for cell in cells]
                down = down + [pltpu.roll(from_right, LANES - 1 - place, 1)]
                results = []
                for tile in range(tiles):
                    at = base + tile
                    mine = plane * tiles + tile
                    near = (
                        cells[tile],
                        now[at - tiles, rows, :],
                        now[at + tiles, rows, :],
                        now[at, pl.ds(row - 1, ROWS), :],
                        now[at, pl.ds(row + 1, ROWS), :],
                        jnp.where(lane == 0, up[tile], up[tile + 1]),
                        jnp.where(lane == LANES - 1, down[tile + 1], down[tile]),
                    )
                    terms = [weight[k, mine, own, :] * near[k] for k in range(7)]
                    total = ((terms[1] + terms[2]) + (terms[3] + terms[4])) + (
                        (terms[5] + terms[6]) + terms[0]
                    )
                    later[at, rows, :] = total
                    results.append(total)
                edges.append((results[0], results[-1]))
            pack(step + 1, group, plane, edges)

            for which in range(4):
                end = starts[which + 1] if which < 3 else CX

                @pl.when(jnp.logical_and(turn == end - 1, step < NSTEP - 1))
                def _():
                    send(later, step + 1, which)

            if final:

                @pl.when(step == NSTEP - 1)
                def _():
                    for tile in range(tiles):
                        pltpu.make_async_copy(
                            later.at[base + tile, body_rows, :],
                            out_ref.at[:, tile_lanes(plane * tiles + tile)],
                            out_sem,
                        ).start()

            return carry

        lax.fori_loop(0, CX, one, 0)

    def two(pair, carry):
        advance(2 * pair, state_a, state_b, False)
        advance(2 * pair + 1, state_b, state_a, True)
        return carry

    lax.fori_loop(0, NSTEP // 2, two, 0)

    for group in range(4):
        z_copy(state_b, NSTEP - 1, group).wait_send()

    def settle(step, carry):
        for side in range(2):
            x_copy(step, side).wait_send()
            for group in range(4):
                y_copy(step, group, side).wait_send()
        return carry

    lax.fori_loop(0, NSTEP, settle, 0)
    each_sum(lambda copy: copy.wait_send(), None)

    @pl.when(fringe)
    def _():
        for peer in peers:
            part_copy(peer).wait_send()
            coef_copy(peer, gy).wait_send()

    pltpu.make_async_copy(whole, whole, out_sem).wait()


def fast_sweep(theta, courants, meso, col_weight, codes, n_gx, n_gy, tile_rows):
    levels = theta.shape[0]
    tiles = tile_rows // LANES
    planes = CX * tiles
    slots = (CX + 2) * tiles
    share = FW // n_gy
    f32, bf16 = jnp.float32, jnp.bfloat16
    field = pltpu.VMEM((slots, levels + 2 * ROWS, LANES), f32)
    faces = pltpu.VMEM((NSTEP, 2, tiles, levels, LANES), bf16)
    lines = pltpu.VMEM((NSTEP + 1, 4, 2, ROWS, LANES), f32)
    dma = pltpu.SemaphoreType.DMA
    anywhere = pl.BlockSpec(memory_space=pl.ANY)
    return pl.pallas_call(
        functools.partial(sweep_kernel, (n_gx, n_gy, levels, tiles)),
        out_shape=jax.ShapeDtypeStruct(theta.shape, f32),
        in_specs=[anywhere] * 5,
        out_specs=anywhere,
        scratch_shapes=[
            field,
            field,
            pltpu.VMEM((7, planes, levels, LANES), f32),
            pltpu.VMEM(courants.shape, bf16),
            pltpu.VMEM(meso.shape, f32),
            pltpu.VMEM(col_weight.shape, f32),
            pltpu.VMEM(codes.shape, jnp.int32),
            pltpu.VMEM((2 * KM, tile_rows), f32),
            pltpu.VMEM((2, ENTRIES, 2 * KM), f32),
            pltpu.VMEM((2 * n_gx, BAND_ROWS, 2 * KM), f32),
            pltpu.VMEM((FW, levels, 2 * KM), f32),
            pltpu.VMEM((n_gy, share, levels, 2 * KM), f32),
            pltpu.VMEM((FW, levels, 2 * KM), bf16),
            faces,
            faces,
            lines,
            lines,
            dma((5,)),
            dma,
            dma((NSTEP, 2)),
            dma((NSTEP, 2)),
            dma((NSTEP, 4, 2)),
            dma((NSTEP, 4, 2)),
            dma((NSTEP, 4)),
            dma((NSTEP, 4)),
            dma((2, 2)),
            dma((2 * n_gx,)),
            dma((n_gy,)),
            dma((n_gy,)),
            dma((n_gy,)),
            dma((n_gy,)),
        ],
        compiler_params=pltpu.CompilerParams(
            collective_id=0, has_side_effects=True, vmem_limit_bytes=58 * 1024 * 1024
        ),
        name="transport",
    )(theta, courants, meso, col_weight, codes)


def body(theta_field, courants, meso_columns, col_weight, owner_ids, line_ids, band_start):
    n_gx, n_gy, n_gz = (lax.axis_size(axis) for axis in ("gx", "gy", "gz"))
    tile_rows = NY // n_gy
    levels = theta_field.shape[2]
    theta_local = theta_field.reshape(levels, CX * tile_rows)
    courant_local = courants.reshape(3, levels, CX * tile_rows)
    column_index = lax.axis_index("gx")
    east_end = column_index == n_gx - 1
    west_end = column_index == 0

    fits = tile_rows % LANES == 0 and levels == 64 and FW % n_gy == 0
    if fits and n_gz == 2 and n_gx > 2 and n_gy > 2:
        result = fast_sweep(
            theta_local,
            courant_local,
            meso_columns,
            col_weight[None, :],
            jnp.stack([owner_ids[:, 0], line_ids, band_start]),
            n_gx,
            n_gy,
            tile_rows,
        )
        return result.reshape(1, 1, levels, CX * tile_rows)

    sums = target_spectrum(meso_columns, col_weight, owner_ids, line_ids, band_start, tile_rows)
    sums = lax.psum(sums, ("gx", "gy", "gz"))
    side_sums = jnp.where(east_end, sums[:, 2 * KM :], sums[:, : 2 * KM])
    bands = lax.dynamic_slice_in_dim(band_matrix(), lax.axis_index("gz") * levels, levels, axis=0)
    target = jnp.dot(bands, side_sums, precision=highest, preferred_element_type=jnp.float32)

    own_waves = waves_at(lax.axis_index("gy") * tile_rows + jnp.arange(tile_rows, dtype=jnp.int32))
    width = FW * tile_rows
    strip = jnp.where(east_end, theta_local[:, -width:], theta_local[:, :width])
    strip = strip.reshape(levels, FW, tile_rows).transpose(1, 0, 2)
    spectrum = jnp.einsum(
        "xky,ym->xkm", strip, own_waves, precision=highest, preferred_element_type=jnp.float32
    )
    spectrum = target[None] - lax.psum(spectrum, "gy")
    offsets = jnp.arange(FW, dtype=jnp.float32)
    relaxation = jnp.where(
        east_end, (offsets + 1.0) / FW, jnp.where(west_end, (FW - offsets) / FW, 0.0)
    )
    coef = spectrum * mode_scale()[None, None, :] * relaxation[:, None, None]

    update = jnp.einsum(
        "xkm,ym->kxy", coef, own_waves, precision=highest, preferred_element_type=jnp.float32
    )
    state_field = theta_local.reshape(levels, CX, tile_rows)
    state_field = jnp.where(
        east_end,
        state_field.at[:, CX - FW :].add(update),
        state_field.at[:, :FW].add(update),
    )
    courant_field = courant_local.reshape(3, levels, CX, tile_rows)
    for step_index in range(NSTEP):
        state_field = sweep_once(state_field, courant_field)
    return state_field.reshape(1, 1, levels, CX * tile_rows)


def solution(mesh):
    in_specs = (
        P("gx", "gy", "gz", None),
        P(None, "gx", "gy", "gz", None),
        P(None, ("gx", "gy", "gz")),
        P(("gx", "gy", "gz")),
        P(("gx", "gy", "gz"), None),
        P(("gx", "gy", "gz")),
        P(("gx", "gy", "gz")),
    )
    out_specs = P("gx", "gy", "gz", None)
    return jax.shard_map(body, mesh=mesh, in_specs=in_specs, out_specs=out_specs, check_vma=False)
```

```python
import functools
import math

import jax
import jax.numpy as jnp
from jax import lax
from jax.experimental import pallas as pl
from jax.experimental.pallas import tpu as pltpu
from jax.sharding import PartitionSpec as P

CX = 16
NY = 3072
ZG = 128
KM = 64
FW = 8
NSTEP = 4
LANES = 128
ROWS = 8

MESH = pl.DeviceIdType.MESH
diffusion = 0.02
highest = lax.Precision.HIGHEST
band_span = 3 * (ZG - 1) // 8 + 2
ENTRIES = 64
BAND_STEP = 24
BAND_ROWS = 32


def extended(array, sides, width, wrap):
    for axis, dim in sides:
        devices, length = (lax.axis_size(axis), array.shape[dim])
        up = [(i, (i + 1) % devices) for i in range(devices if wrap else devices - 1)]
        down = [(j, i) for i, j in up]
        last = lax.slice_in_dim(array, length - width, length, axis=dim)
        initial = lax.slice_in_dim(array, 0, width, axis=dim)
        before = lax.ppermute(last, axis, up)
        after = lax.ppermute(initial, axis, down)
        array = jnp.concatenate([before, array, after], axis=dim)
    return array


def band_matrix():
    levels_z = jnp.arange(ZG, dtype=jnp.int32)
    lower_index = 3 * levels_z // 8
    fraction = (3 * levels_z % 8).astype(jnp.float32) / 8.0
    entries = jnp.arange(band_span, dtype=jnp.int32)[None, :]
    return (1.0 - fraction)[:, None] * (entries == lower_index[:, None]) + fraction[:, None] * (
        entries == lower_index[:, None] + 1
    )


def waves_at(places):
    numbers = jnp.arange(KM, dtype=jnp.int32)
    phases = places[:, None] * numbers[None, :] % NY
    angles = phases.astype(jnp.float32) * (2.0 * math.pi / NY)
    return jnp.concatenate([jnp.cos(angles), jnp.sin(angles)], axis=1)


def mode_scale():
    return jnp.where(jnp.arange(2 * KM, dtype=jnp.int32) % KM == 0, 1.0 / NY, 2.0 / NY).astype(
        jnp.float32
    )


def upwind(state_field, courant_one, ahead_cell, behind_cell):
    return -jnp.maximum(courant_one, 0.0) * (state_field - behind_cell) - jnp.minimum(
        courant_one, 0.0
    ) * (ahead_cell - state_field)


def sweep_once(state_field, courant_local):
    side_cells = extended(state_field, (("gx", 1), ("gy", 2)), 1, True)
    level_cells = extended(state_field, (("gz", 0),), 1, False)
    pairs = (
        (side_cells[:, 2:, 1:-1], side_cells[:, :-2, 1:-1]),
        (level_cells[2:], level_cells[:-2]),
        (side_cells[:, 1:-1, 2:], side_cells[:, 1:-1, :-2]),
    )
    change = 0.0
    neighbours = 0.0
    for direction, (ahead, behind) in enumerate(pairs):
        change = change + upwind(
            state_field, courant_local[direction].astype(jnp.float32), ahead, behind
        )
        neighbours = neighbours + ahead + behind
    return state_field + change + diffusion * (neighbours - 6.0 * state_field)


def target_spectrum(meso_columns, col_weight, owner_ids, line_ids, band_start, tile_rows):
    owners = owner_ids[:, 0]
    places = owners // 2 * tile_rows + line_ids
    waves = waves_at(places) * col_weight[:, None]
    sided = jnp.concatenate(
        [jnp.where((owners % 2 == side)[:, None], waves, 0.0) for side in range(2)], axis=1
    )
    shifted = jnp.zeros((band_span, meso_columns.shape[1]), jnp.float32)
    for offset in range(meso_columns.shape[0] - band_span + 1):
        shifted = shifted + jnp.where(
            band_start[None, :] == offset, meso_columns[offset : offset + band_span], 0.0
        )
    return jnp.dot(shifted, sided, precision=highest, preferred_element_type=jnp.float32)


def waves_of(places):
    numbers = lax.broadcasted_iota(jnp.int32, (KM, places.shape[1]), 0).astype(jnp.float32)
    turns = numbers * places
    quarter = NY // 4
    quarters = jnp.floor(turns * (1.0 / quarter) + 0.5)
    angle = (turns - quarter * quarters) * (2.0 * math.pi / NY)
    square = angle * angle
    sine = 1.0 / 362880.0
    for factor in (-1.0 / 5040.0, 1.0 / 120.0, -1.0 / 6.0, 1.0):
        sine = sine * square + factor
    sine = sine * angle
    cosine = 1.0 / 40320.0
    for factor in (-1.0 / 720.0, 1.0 / 24.0, -0.5, 1.0):
        cosine = cosine * square + factor
    corner = quarters - 4.0 * jnp.floor(quarters * 0.25)
    odd = jnp.logical_or(corner == 1.0, corner == 3.0)
    cos_values = jnp.where(odd, sine, cosine)
    sin_values = jnp.where(odd, cosine, sine)
    cos_values = jnp.where(
        jnp.logical_or(corner == 1.0, corner == 2.0), -cos_values, cos_values
    )
    sin_values = jnp.where(corner >= 2.0, -sin_values, sin_values)
    return jnp.concatenate([cos_values, sin_values], axis=0)


def in_two(values):
    high = values.astype(jnp.bfloat16)
    return high, (values - high.astype(jnp.float32)).astype(jnp.bfloat16)


def dot_two(left, right, dims):
    def one(a, b):
        return lax.dot_general(a, b, (dims, ((), ())), preferred_element_type=jnp.float32)

    return one(left[0], right[0]) + (one(left[1], right[0]) + one(left[0], right[1]))


def sweep_kernel(
    sizes,
    theta_ref,
    courant_ref,
    meso_ref,
    col_weight_ref,
    codes_ref,
    out_ref,
    state_a,
    state_b,
    weight,
    courant,
    meso,
    col_weight,
    codes,
    waves_to,
    waves_back,
    strips,
    sum_send,
    sum_recv,
    part,
    part_recv,
    coef,
    x_send,
    x_recv,
    y_send,
    y_recv,
    in_sem,
    out_sem,
    xs_sem,
    xr_sem,
    ys_sem,
    yr_sem,
    zs_sem,
    zr_sem,
    ss_sem,
    sr_sem,
    ps_sem,
    pr_sem,
    cs_sem,
    cr_sem,
):
    n_gx, n_gy, levels, tiles = sizes
    chunks = levels // ROWS
    planes = CX * tiles
    gx, gy, gz = (lax.axis_index(axis) for axis in ("gx", "gy", "gz"))
    x_right, x_left = lax.rem(gx + 1, n_gx), lax.rem(gx + n_gx - 1, n_gx)
    y_right, y_left = lax.rem(gy + 1, n_gy), lax.rem(gy + n_gy - 1, n_gy)
    other = 1 - gz
    east_end = gx == n_gx - 1
    west_end = gx == 0
    body_rows = pl.ds(ROWS, levels)

    def tile_lanes(tile):
        return pl.ds(pl.multiple_of(tile * LANES, LANES), LANES)

    courant_copy = pltpu.make_async_copy(courant_ref, courant, in_sem.at[1])
    column_copies = [
        pltpu.make_async_copy(meso_ref, meso, in_sem.at[2]),
        pltpu.make_async_copy(col_weight_ref, col_weight, in_sem.at[3]),
        pltpu.make_async_copy(codes_ref, codes, in_sem.at[4]),
    ]

    def fetch(tile, carry):
        pltpu.make_async_copy(
            theta_ref.at[:, tile_lanes(tile)],
            state_a.at[tile + tiles, body_rows, :],
            in_sem.at[0],
        ).start()
        return carry

    for copy in column_copies:
        copy.start()
    lax.fori_loop(0, planes, fetch, 0)
    courant_copy.start()

    barrier = pltpu.get_barrier_semaphore()
    greeted = 0
    for step_x in range(n_gx):
        for step_z in range(2):
            if step_x + step_z > 0:
                friend = {"gx": lax.rem(gx + step_x, n_gx), "gz": lax.rem(gz + step_z, 2)}
                pl.semaphore_signal(barrier, inc=1, device_id=friend, device_id_type=MESH)
                greeted += 1
    for step_y in range(1, n_gy):
        friend = {"gy": lax.rem(gy + step_y, n_gy)}
        pl.semaphore_signal(barrier, inc=1, device_id=friend, device_id_type=MESH)
        greeted += 1

    tile_rows = tiles * LANES
    row_places = lax.broadcasted_iota(jnp.int32, (1, tile_rows), 1) + gy * tile_rows
    row_waves = waves_of(row_places.astype(jnp.float32))
    for piece, values in enumerate(in_two(row_waves)):
        waves_back[piece * 2 * KM : (piece + 1) * 2 * KM, :] = values
    for piece, values in enumerate(in_two(row_waves.T)):
        waves_to[piece] = values
    for copy in column_copies:
        copy.wait()
    owners, lines, bands = codes[0:1, :], codes[1:2, :], codes[2:3, :]
    column_count = meso.shape[1]
    places = jnp.right_shift(owners, 1) * tile_rows + lines
    column_waves = waves_of(places.astype(jnp.float32))
    entries = meso.shape[0]
    shifted = jnp.concatenate(
        [meso[...], jnp.zeros((ENTRIES - entries, column_count), jnp.float32)], axis=0
    )
    for bit in range(4):
        moved = pltpu.roll(shifted, ENTRIES - (1 << bit), 0)
        chosen = jnp.bitwise_and(jnp.right_shift(bands, bit), 1) == 1
        shifted = jnp.where(chosen, moved, shifted)
    sides = [
        shifted * jnp.where(jnp.bitwise_and(owners, 1) == side, col_weight[...], 0.0)
        for side in range(2)
    ]
    sums = dot_two(
        in_two(jnp.concatenate(sides, axis=0)), in_two(column_waves), ((1,), (1,))
    )
    sum_send[0] = sums[:ENTRIES]
    sum_send[1] = sums[ENTRIES:]

    pl.semaphore_wait(barrier, greeted)

    def sum_copy(side, half_z):
        return pltpu.make_async_remote_copy(
            src_ref=sum_send.at[side, pl.ds(BAND_STEP * half_z, BAND_ROWS), :],
            dst_ref=sum_recv.at[2 * gx + gz],
            send_sem=ss_sem.at[side, half_z],
            recv_sem=sr_sem.at[2 * gx + gz],
            device_id={"gx": side * (n_gx - 1), "gz": half_z},
            device_id_type=MESH,
        )

    def each_sum(act, act_here):
        for side in range(2):
            for half_z in range(2):
                here = jnp.logical_and(gx == side * (n_gx - 1), gz == half_z)

                @pl.when(jnp.logical_not(here))
                def _():
                    act(sum_copy(side, half_z))

                if act_here is not None:

                    @pl.when(here)
                    def _():
                        act_here(side, half_z)

    def keep_sum(side, half_z):
        start = BAND_STEP * half_z
        sum_recv[2 * gx + gz] = sum_send[side, start : start + BAND_ROWS, :]

    each_sum(lambda copy: copy.start(), keep_sum)

    zero_rows = pl.ds(pl.multiple_of(jnp.where(gz == 0, 0, ROWS + levels), ROWS), ROWS)

    def blank(tile, carry):
        for state in (state_a, state_b):
            state[tile + tiles, zero_rows, :] = jnp.zeros((ROWS, LANES), jnp.float32)
        return carry

    lax.fori_loop(0, planes, blank, 0)
    y_send[...] = jnp.zeros_like(y_send)
    lane = lax.broadcasted_iota(jnp.int32, (ROWS, LANES), 1)

    whole = state_a.at[pl.ds(tiles, planes), body_rows, :]
    pltpu.make_async_copy(whole, whole, in_sem.at[0]).wait()

    part_rows = levels // 2

    def x_copy(step, side, piece):
        target = jnp.where(side == 0, x_right, x_left)
        return pltpu.make_async_remote_copy(
            src_ref=x_send.at[step, side, piece],
            dst_ref=x_recv.at[step, side, piece],
            send_sem=xs_sem.at[step, side, piece],
            recv_sem=xr_sem.at[step, side, piece],
            device_id={"gx": target},
            device_id_type=MESH,
        )

    def send_face(state, step, side, piece):
        base = ((1 - side) * (CX - 1) + 1) * tiles
        rows = pl.ds(ROWS + piece * part_rows, part_rows)
        for tile in range(tiles):
            x_send[step, side, piece, tile] = state[base + tile, rows, :].astype(jnp.bfloat16)
        x_copy(step, side, piece).start()

    def send_faces(side):
        for piece in range(2):
            send_face(state_a, 0, side, piece)

    @pl.when(jnp.logical_not(east_end))
    def _():
        send_faces(0)

    @pl.when(jnp.logical_not(west_end))
    def _():
        send_faces(1)

    fringe = jnp.logical_or(west_end, east_end)
    first = jnp.where(east_end, CX - FW, 0)
    share = FW // n_gy

    def part_copy(peer):
        return pltpu.make_async_remote_copy(
            src_ref=part.at[pl.ds(peer * share, share)],
            dst_ref=part_recv.at[gy],
            send_sem=ps_sem.at[peer],
            recv_sem=pr_sem.at[gy],
            device_id={"gy": peer},
            device_id_type=MESH,
        )

    def part_arrival(peer):
        return pltpu.make_async_remote_copy(
            src_ref=part.at[pl.ds(peer * share, share)],
            dst_ref=part_recv.at[peer],
            send_sem=ps_sem.at[peer],
            recv_sem=pr_sem.at[peer],
            device_id={"gy": peer},
            device_id_type=MESH,
        )

    def coef_copy(peer, owner):
        return pltpu.make_async_remote_copy(
            src_ref=coef.at[pl.ds(owner * share, share)],
            dst_ref=coef.at[pl.ds(owner * share, share)],
            send_sem=cs_sem.at[peer],
            recv_sem=cr_sem.at[owner],
            device_id={"gy": peer},
            device_id_type=MESH,
        )

    peers = [lax.rem(gy + step_y, n_gy) for step_y in range(1, n_gy)]

    @pl.when(fringe)
    def _():
        def strip_spectrum(index, carry):
            base = (first + index + 1) * tiles
            strip = jnp.concatenate(
                [state_a[base + tile, body_rows, :] for tile in range(tiles)], axis=1
            )
            at = pl.ds(pl.multiple_of(index * levels, levels), levels)
            for piece, values in enumerate(in_two(strip)):
                strips[piece, at, :] = values
            return carry

        lax.fori_loop(0, FW, strip_spectrum, 0)
        spectrum = dot_two(
            (strips[0], strips[1]), (waves_to[0], waves_to[1]), ((1,), (0,))
        )
        part[...] = spectrum.reshape(part.shape)

        total = jnp.zeros((BAND_ROWS, 2 * KM), jnp.float32)
        for slot in range(2 * n_gx):

            @pl.when(slot != 2 * gx + gz)
            def _():
                pltpu.make_async_remote_copy(
                    src_ref=sum_send.at[0, pl.ds(0, BAND_ROWS), :],
                    dst_ref=sum_recv.at[slot],
                    send_sem=ss_sem.at[0, 0],
                    recv_sem=sr_sem.at[slot],
                    device_id={"gz": other},
                    device_id_type=MESH,
                ).wait_recv()

        for slot in range(2 * n_gx):
            total = total + sum_recv[slot]
        level = lax.broadcasted_iota(jnp.int32, (levels, BAND_ROWS), 0) + gz * levels
        entry = lax.broadcasted_iota(jnp.int32, (levels, BAND_ROWS), 1) + gz * BAND_STEP
        lower = jnp.right_shift(3 * level, 3)
        fraction = jnp.bitwise_and(3 * level, 7).astype(jnp.float32) * 0.125
        band = jnp.where(entry == lower, 1.0 - fraction, 0.0) + jnp.where(
            entry == lower + 1, fraction, 0.0
        )
        target = jnp.dot(band, total, precision=highest, preferred_element_type=jnp.float32)

        def subtract(index, carry):
            part[index] = target - part[index]
            return carry

        lax.fori_loop(0, FW, subtract, 0)
        for peer in peers:
            part_copy(peer).start()

    courant_copy.wait()

    def weigh(tile, carry):
        centre = 1.0
        for direction in range(3):
            number = courant[direction, :, tile_lanes(tile)].astype(jnp.float32)
            upward = jnp.maximum(number, 0.0)
            behind = upward + diffusion
            ahead = (upward - number) + diffusion
            weight[2 * direction + 1, tile] = behind
            weight[2 * direction + 2, tile] = ahead
            centre = centre - (behind + ahead)
        weight[0, tile] = centre
        return carry

    lax.fori_loop(0, planes, weigh, 0)

    @pl.when(fringe)
    def _():
        for peer in peers:
            part_arrival(peer).wait_recv()
        mode = lax.broadcasted_iota(jnp.int32, (levels, 2 * KM), 1)
        scale = jnp.where(jnp.bitwise_and(mode, KM - 1) == 0, 1.0 / NY, 2.0 / NY)
        for index in range(share):
            plane = gy * share + index
            total = part[plane]
            for peer in peers:
                total = total + part_recv[peer, index]
            steps = jnp.where(east_end, plane + 1, FW - plane).astype(jnp.float32)
            coef[plane] = (total * (scale * (steps * (1.0 / FW)))).astype(jnp.bfloat16)
        for peer in peers:
            coef_copy(peer, gy).start()
        for peer in peers:
            coef_copy(peer, peer).wait_recv()

        both = coef[...].reshape(FW * levels, 2 * KM)
        both = jnp.concatenate([both, both], axis=1)
        for start in range(0, tiles, 2):
            stop = min(start + 2, tiles)
            smooth = jnp.dot(
                both,
                waves_back[:, start * LANES : stop * LANES],
                preferred_element_type=jnp.float32,
            )
            for index in range(FW):
                own = slice(index * levels, (index + 1) * levels)
                for tile in range(start, stop):
                    at = (first + index + 1) * tiles + tile
                    where = slice((tile - start) * LANES, (tile - start + 1) * LANES)
                    state_a[at, body_rows, :] += smooth[own, where]

    @pl.when(east_end)
    def _():
        send_faces(0)

    @pl.when(west_end)
    def _():
        send_faces(1)

    source_rows = pl.ds(pl.multiple_of(jnp.where(gz == 0, levels, ROWS), ROWS), ROWS)
    target_rows = pl.ds(pl.multiple_of(jnp.where(gz == 0, 0, ROWS + levels), ROWS), ROWS)

    def z_copy(state, step, group):
        first, count = groups[group]
        some = pl.ds((first + 1) * tiles, count * tiles)
        return pltpu.make_async_remote_copy(
            src_ref=state.at[some, source_rows, :],
            dst_ref=state.at[some, target_rows, :],
            send_sem=zs_sem.at[step, group],
            recv_sem=zr_sem.at[step, group],
            device_id={"gz": other},
            device_id_type=MESH,
        )

    def y_copy(step, group, side):
        return pltpu.make_async_remote_copy(
            src_ref=y_send.at[step, group, side],
            dst_ref=y_recv.at[step, group, side],
            send_sem=ys_sem.at[step, group, side],
            recv_sem=yr_sem.at[step, group, side],
            device_id={"gy": y_right if side == 0 else y_left},
            device_id_type=MESH,
        )

    half = (CX - 2) // 2
    groups = ((1, half), (1 + half, half), (0, 1), (CX - 1, 1))

    def pack(step, group, plane, edges):
        right, left = y_send[step, group, 0], y_send[step, group, 1]
        for chunk, low, high in edges:
            place = plane + chunk * CX
            here = lane == place
            right = jnp.where(here, pltpu.roll(high, lax.rem(place + 1, LANES), 1), right)
            left = jnp.where(here, pltpu.roll(low, place, 1), left)
        y_send[step, group, 0] = right
        y_send[step, group, 1] = left

    def send(state, step, group):
        z_copy(state, step, group).start()
        for side in range(2):
            y_copy(step, group, side).start()

    def pack_planes(group):
        first_plane, count = groups[group]

        def pack_start(plane, carry):
            base = (plane + 1) * tiles
            edges = []
            for chunk in range(chunks):
                rows = pl.ds(ROWS + chunk * ROWS, ROWS)
                edges.append((chunk, state_a[base, rows, :], state_a[base + tiles - 1, rows, :]))
            pack(0, group, plane, edges)
            return carry

        lax.fori_loop(first_plane, first_plane + count, pack_start, 0)
        send(state_a, 0, group)

    for group in range(4):
        pack_planes(group)

    def advance(step, now, later, final):
        going_on = step < NSTEP - 1

        def arrive(group):
            z_copy(now, step, group).wait_recv()
            for side in range(2):
                y_copy(step, group, side).wait_recv()

            @pl.when(step > 0)
            def _():
                z_copy(later, step - 1, group).wait_send()

        def send_next(group):
            @pl.when(going_on)
            def _():
                send(later, step + 1, group)

        def put_out(plane):
            if final:

                @pl.when(step == NSTEP - 1)
                def _():
                    for tile in range(tiles):
                        pltpu.make_async_copy(
                            later.at[(plane + 1) * tiles + tile, body_rows, :],
                            out_ref.at[:, tile_lanes(plane * tiles + tile)],
                            out_sem,
                        ).start()

        def move(plane, group, some):
            base = (plane + 1) * tiles
            from_left = y_recv[step, group, 0]
            from_right = y_recv[step, group, 1]
            edges = []
            for chunk in some:
                row = ROWS + chunk * ROWS
                rows = pl.ds(row, ROWS)
                own = pl.ds(chunk * ROWS, ROWS)
                place = plane + chunk * CX
                cells = [now[base + tile, rows, :] for tile in range(tiles)]
                up = [pltpu.roll(from_left, lax.rem(LANES - place, LANES), 1)]
                up = up + [pltpu.roll(cell, 1, 1) for cell in cells]
                down = [pltpu.roll(cell, LANES - 1, 1) for cell in cells]
                down = down + [pltpu.roll(from_right, LANES - 1 - place, 1)]
                results = []
                for tile in range(tiles):
                    at = base + tile
                    mine = plane * tiles + tile
                    near = (
                        cells[tile],
                        now[at - tiles, rows, :],
                        now[at + tiles, rows, :],
                        now[at, pl.ds(row - 1, ROWS), :],
                        now[at, pl.ds(row + 1, ROWS), :],
                        jnp.where(lane == 0, up[tile], up[tile + 1]),
                        jnp.where(lane == LANES - 1, down[tile + 1], down[tile]),
                    )
                    terms = [weight[k, mine, own, :] * near[k] for k in range(7)]
                    total = ((terms[1] + terms[2]) + (terms[3] + terms[4])) + (
                        (terms[5] + terms[6]) + terms[0]
                    )
                    later[at, rows, :] = total
                    results.append(total)
                edges.append((chunk, results[0], results[-1]))
            pack(step + 1, group, plane, edges)

        for piece in range(2):
            arrive(piece)
            first_plane, count = groups[piece]

            def inner(plane, carry):
                move(plane, piece, range(chunks))
                put_out(plane)
                return carry

            lax.fori_loop(first_plane, first_plane + count, inner, 0)
            send_next(piece)
            if piece == 0:
                arrive(2)
                arrive(3)
            some = range(piece * chunks // 2, (piece + 1) * chunks // 2)
            rows = pl.ds(ROWS + piece * part_rows, part_rows)

            def edge(end, carry):
                plane = end * (CX - 1)
                x_copy(step, end, piece).wait_recv()
                base = end * (CX + 1) * tiles
                for tile in range(tiles):
                    now[base + tile, rows, :] = x_recv[step, end, piece, tile].astype(jnp.float32)
                move(plane, 2 + end, some)

                @pl.when(going_on)
                def _():
                    send_face(later, step + 1, 1 - end, piece)

                if piece == 1:
                    put_out(plane)
                return carry

            lax.fori_loop(0, 2, edge, 0)
        send_next(2)
        send_next(3)

    def two(pair, carry):
        advance(2 * pair, state_a, state_b, False)
        advance(2 * pair + 1, state_b, state_a, True)
        return carry

    lax.fori_loop(0, NSTEP // 2, two, 0)

    for group in range(4):
        z_copy(state_b, NSTEP - 1, group).wait_send()

    def settle(step, carry):
        for side in range(2):
            for piece in range(2):
                x_copy(step, side, piece).wait_send()
            for group in range(4):
                y_copy(step, group, side).wait_send()
        return carry

    lax.fori_loop(0, NSTEP, settle, 0)
    each_sum(lambda copy: copy.wait_send(), None)

    @pl.when(fringe)
    def _():
        for peer in peers:
            part_copy(peer).wait_send()
            coef_copy(peer, gy).wait_send()

    pltpu.make_async_copy(whole, whole, out_sem).wait()


def fast_sweep(theta, courants, meso, col_weight, codes, n_gx, n_gy, tile_rows):
    levels = theta.shape[0]
    tiles = tile_rows // LANES
    planes = CX * tiles
    slots = (CX + 2) * tiles
    share = FW // n_gy
    f32, bf16 = jnp.float32, jnp.bfloat16
    field = pltpu.VMEM((slots, levels + 2 * ROWS, LANES), f32)
    faces = pltpu.VMEM((NSTEP, 2, 2, tiles, levels // 2, LANES), bf16)
    lines = pltpu.VMEM((NSTEP + 1, 4, 2, ROWS, LANES), f32)
    dma = pltpu.SemaphoreType.DMA
    anywhere = pl.BlockSpec(memory_space=pl.ANY)
    return pl.pallas_call(
        functools.partial(sweep_kernel, (n_gx, n_gy, levels, tiles)),
        out_shape=jax.ShapeDtypeStruct(theta.shape, f32),
        in_specs=[anywhere] * 5,
        out_specs=anywhere,
        scratch_shapes=[
            field,
            field,
            pltpu.VMEM((7, planes, levels, LANES), f32),
            pltpu.VMEM(courants.shape, bf16),
            pltpu.VMEM(meso.shape, f32),
            pltpu.VMEM(col_weight.shape, f32),
            pltpu.VMEM(codes.shape, jnp.int32),
            pltpu.VMEM((2, tile_rows, 2 * KM), bf16),
            pltpu.VMEM((4 * KM, tile_rows), bf16),
            pltpu.VMEM((2, FW * levels, tile_rows), bf16),
            pltpu.VMEM((2, ENTRIES, 2 * KM), f32),
            pltpu.VMEM((2 * n_gx, BAND_ROWS, 2 * KM), f32),
            pltpu.VMEM((FW, levels, 2 * KM), f32),
            pltpu.VMEM((n_gy, share, levels, 2 * KM), f32),
            pltpu.VMEM((FW, levels, 2 * KM), bf16),
            faces,
            faces,
            lines,
            lines,
            dma((5,)),
            dma,
            dma((NSTEP, 2, 2)),
            dma((NSTEP, 2, 2)),
            dma((NSTEP, 4, 2)),
            dma((NSTEP, 4, 2)),
            dma((NSTEP, 4)),
            dma((NSTEP, 4)),
            dma((2, 2)),
            dma((2 * n_gx,)),
            dma((n_gy,)),
            dma((n_gy,)),
            dma((n_gy,)),
            dma((n_gy,)),
        ],
        compiler_params=pltpu.CompilerParams(
            collective_id=0, has_side_effects=True, vmem_limit_bytes=58 * 1024 * 1024
        ),
        name="transport",
    )(theta, courants, meso, col_weight, codes)


def body(theta_field, courants, meso_columns, col_weight, owner_ids, line_ids, band_start):
    n_gx, n_gy, n_gz = (lax.axis_size(axis) for axis in ("gx", "gy", "gz"))
    tile_rows = NY // n_gy
    levels = theta_field.shape[2]
    theta_local = theta_field.reshape(levels, CX * tile_rows)
    courant_local = courants.reshape(3, levels, CX * tile_rows)
    column_index = lax.axis_index("gx")
    east_end = column_index == n_gx - 1
    west_end = column_index == 0

    fits = tile_rows % LANES == 0 and levels == 64 and FW % n_gy == 0
    if fits and n_gz == 2 and n_gx > 2 and n_gy > 2:
        result = fast_sweep(
            theta_local,
            courant_local,
            meso_columns,
            col_weight[None, :],
            jnp.stack([owner_ids[:, 0], line_ids, band_start]),
            n_gx,
            n_gy,
            tile_rows,
        )
        return result.reshape(1, 1, levels, CX * tile_rows)

    sums = target_spectrum(meso_columns, col_weight, owner_ids, line_ids, band_start, tile_rows)
    sums = lax.psum(sums, ("gx", "gy", "gz"))
    side_sums = jnp.where(east_end, sums[:, 2 * KM :], sums[:, : 2 * KM])
    bands = lax.dynamic_slice_in_dim(band_matrix(), lax.axis_index("gz") * levels, levels, axis=0)
    target = jnp.dot(bands, side_sums, precision=highest, preferred_element_type=jnp.float32)

    own_waves = waves_at(lax.axis_index("gy") * tile_rows + jnp.arange(tile_rows, dtype=jnp.int32))
    width = FW * tile_rows
    strip = jnp.where(east_end, theta_local[:, -width:], theta_local[:, :width])
    strip = strip.reshape(levels, FW, tile_rows).transpose(1, 0, 2)
    spectrum = jnp.einsum(
        "xky,ym->xkm", strip, own_waves, precision=highest, preferred_element_type=jnp.float32
    )
    spectrum = target[None] - lax.psum(spectrum, "gy")
    offsets = jnp.arange(FW, dtype=jnp.float32)
    relaxation = jnp.where(
        east_end, (offsets + 1.0) / FW, jnp.where(west_end, (FW - offsets) / FW, 0.0)
    )
    coef = spectrum * mode_scale()[None, None, :] * relaxation[:, None, None]

    update = jnp.einsum(
        "xkm,ym->kxy", coef, own_waves, precision=highest, preferred_element_type=jnp.float32
    )
    state_field = theta_local.reshape(levels, CX, tile_rows)
    state_field = jnp.where(
        east_end,
        state_field.at[:, CX - FW :].add(update),
        state_field.at[:, :FW].add(update),
    )
    courant_field = courant_local.reshape(3, levels, CX, tile_rows)
    for step_index in range(NSTEP):
        state_field = sweep_once(state_field, courant_field)
    return state_field.reshape(1, 1, levels, CX * tile_rows)


def solution(mesh):
    in_specs = (
        P("gx", "gy", "gz", None),
        P(None, "gx", "gy", "gz", None),
        P(None, ("gx", "gy", "gz")),
        P(("gx", "gy", "gz")),
        P(("gx", "gy", "gz"), None),
        P(("gx", "gy", "gz")),
        P(("gx", "gy", "gz")),
    )
    out_specs = P("gx", "gy", "gz", None)
    return jax.shard_map(body, mesh=mesh, in_specs=in_specs, out_specs=out_specs, check_vma=False)
```

```python
import functools
import math

import jax
import jax.numpy as jnp
from jax import lax
from jax.experimental import pallas as pl
from jax.experimental.pallas import tpu as pltpu
from jax.sharding import PartitionSpec as P

CX = 16
NY = 3072
ZG = 128
KM = 64
FW = 8
NSTEP = 4
LANES = 128
ROWS = 8

MESH = pl.DeviceIdType.MESH
diffusion = 0.02
highest = lax.Precision.HIGHEST
band_span = 3 * (ZG - 1) // 8 + 2
ENTRIES = 64
BAND_STEP = 24
BAND_ROWS = 32


def extended(array, sides, width, wrap):
    for axis, dim in sides:
        devices, length = (lax.axis_size(axis), array.shape[dim])
        up = [(i, (i + 1) % devices) for i in range(devices if wrap else devices - 1)]
        down = [(j, i) for i, j in up]
        last = lax.slice_in_dim(array, length - width, length, axis=dim)
        initial = lax.slice_in_dim(array, 0, width, axis=dim)
        before = lax.ppermute(last, axis, up)
        after = lax.ppermute(initial, axis, down)
        array = jnp.concatenate([before, array, after], axis=dim)
    return array


def band_matrix():
    levels_z = jnp.arange(ZG, dtype=jnp.int32)
    lower_index = 3 * levels_z // 8
    fraction = (3 * levels_z % 8).astype(jnp.float32) / 8.0
    entries = jnp.arange(band_span, dtype=jnp.int32)[None, :]
    return (1.0 - fraction)[:, None] * (entries == lower_index[:, None]) + fraction[:, None] * (
        entries == lower_index[:, None] + 1
    )


def waves_at(places):
    numbers = jnp.arange(KM, dtype=jnp.int32)
    phases = places[:, None] * numbers[None, :] % NY
    angles = phases.astype(jnp.float32) * (2.0 * math.pi / NY)
    return jnp.concatenate([jnp.cos(angles), jnp.sin(angles)], axis=1)


def mode_scale():
    return jnp.where(jnp.arange(2 * KM, dtype=jnp.int32) % KM == 0, 1.0 / NY, 2.0 / NY).astype(
        jnp.float32
    )


def upwind(state_field, courant_one, ahead_cell, behind_cell):
    return -jnp.maximum(courant_one, 0.0) * (state_field - behind_cell) - jnp.minimum(
        courant_one, 0.0
    ) * (ahead_cell - state_field)


def sweep_once(state_field, courant_local):
    side_cells = extended(state_field, (("gx", 1), ("gy", 2)), 1, True)
    level_cells = extended(state_field, (("gz", 0),), 1, False)
    pairs = (
        (side_cells[:, 2:, 1:-1], side_cells[:, :-2, 1:-1]),
        (level_cells[2:], level_cells[:-2]),
        (side_cells[:, 1:-1, 2:], side_cells[:, 1:-1, :-2]),
    )
    change = 0.0
    neighbours = 0.0
    for direction, (ahead, behind) in enumerate(pairs):
        change = change + upwind(
            state_field, courant_local[direction].astype(jnp.float32), ahead, behind
        )
        neighbours = neighbours + ahead + behind
    return state_field + change + diffusion * (neighbours - 6.0 * state_field)


def target_spectrum(meso_columns, col_weight, owner_ids, line_ids, band_start, tile_rows):
    owners = owner_ids[:, 0]
    places = owners // 2 * tile_rows + line_ids
    waves = waves_at(places) * col_weight[:, None]
    sided = jnp.concatenate(
        [jnp.where((owners % 2 == side)[:, None], waves, 0.0) for side in range(2)], axis=1
    )
    shifted = jnp.zeros((band_span, meso_columns.shape[1]), jnp.float32)
    for offset in range(meso_columns.shape[0] - band_span + 1):
        shifted = shifted + jnp.where(
            band_start[None, :] == offset, meso_columns[offset : offset + band_span], 0.0
        )
    return jnp.dot(shifted, sided, precision=highest, preferred_element_type=jnp.float32)


def waves_of(places):
    numbers = lax.broadcasted_iota(jnp.int32, (KM, places.shape[1]), 0).astype(jnp.float32)
    turns = numbers * places
    quarter = NY // 4
    quarters = jnp.floor(turns * (1.0 / quarter) + 0.5)
    angle = (turns - quarter * quarters) * (2.0 * math.pi / NY)
    square = angle * angle
    sine = 1.0 / 362880.0
    for factor in (-1.0 / 5040.0, 1.0 / 120.0, -1.0 / 6.0, 1.0):
        sine = sine * square + factor
    sine = sine * angle
    cosine = 1.0 / 40320.0
    for factor in (-1.0 / 720.0, 1.0 / 24.0, -0.5, 1.0):
        cosine = cosine * square + factor
    corner = quarters - 4.0 * jnp.floor(quarters * 0.25)
    odd = jnp.logical_or(corner == 1.0, corner == 3.0)
    cos_values = jnp.where(odd, sine, cosine)
    sin_values = jnp.where(odd, cosine, sine)
    cos_values = jnp.where(
        jnp.logical_or(corner == 1.0, corner == 2.0), -cos_values, cos_values
    )
    sin_values = jnp.where(corner >= 2.0, -sin_values, sin_values)
    return jnp.concatenate([cos_values, sin_values], axis=0)


def in_two(values):
    high = values.astype(jnp.bfloat16)
    return high, (values - high.astype(jnp.float32)).astype(jnp.bfloat16)


def dot_two(left, right, dims):
    def one(a, b):
        return lax.dot_general(a, b, (dims, ((), ())), preferred_element_type=jnp.float32)

    return one(left[0], right[0]) + (one(left[1], right[0]) + one(left[0], right[1]))


def sweep_kernel(
    sizes,
    theta_ref,
    courant_ref,
    meso_ref,
    col_weight_ref,
    owner_ref,
    line_ref,
    band_ref,
    out_ref,
    state_a,
    state_b,
    weight,
    courant,
    meso,
    col_weight,
    owner_ids,
    line_ids,
    band_ids,
    waves_to,
    waves_back,
    strips,
    sum_send,
    sum_recv,
    part,
    part_recv,
    coef,
    x_send,
    x_recv,
    y_send,
    y_recv,
    in_sem,
    xs_sem,
    xr_sem,
    ys_sem,
    yr_sem,
    zs_sem,
    zr_sem,
    ss_sem,
    sr_sem,
    ps_sem,
    pr_sem,
    cs_sem,
    cr_sem,
):
    n_gx, n_gy, levels, tiles = sizes
    chunks = levels // ROWS
    planes = CX * tiles
    gx, gy, gz = (lax.axis_index(axis) for axis in ("gx", "gy", "gz"))
    x_right, x_left = lax.rem(gx + 1, n_gx), lax.rem(gx + n_gx - 1, n_gx)
    y_right, y_left = lax.rem(gy + 1, n_gy), lax.rem(gy + n_gy - 1, n_gy)
    other = 1 - gz
    east_end = gx == n_gx - 1
    west_end = gx == 0
    body_rows = pl.ds(ROWS, levels)

    def tile_lanes(tile):
        return pl.ds(pl.multiple_of(tile * LANES, LANES), LANES)

    courant_copy = pltpu.make_async_copy(courant_ref, courant, in_sem.at[1])
    column_copies = [
        pltpu.make_async_copy(meso_ref, meso, in_sem.at[2]),
        pltpu.make_async_copy(col_weight_ref, col_weight, in_sem.at[3]),
        pltpu.make_async_copy(owner_ref, owner_ids, in_sem.at[4]),
        pltpu.make_async_copy(line_ref, line_ids, in_sem.at[5]),
        pltpu.make_async_copy(band_ref, band_ids, in_sem.at[6]),
    ]

    def fetch(tile, carry):
        pltpu.make_async_copy(
            theta_ref.at[:, tile_lanes(tile)],
            state_a.at[tile + tiles, body_rows, :],
            in_sem.at[0],
        ).start()
        return carry

    barrier = pltpu.get_barrier_semaphore()
    greeted = 0
    for step_x in range(n_gx):
        for step_z in range(2):
            if step_x + step_z > 0:
                friend = {"gx": lax.rem(gx + step_x, n_gx), "gz": lax.rem(gz + step_z, 2)}
                pl.semaphore_signal(barrier, inc=1, device_id=friend, device_id_type=MESH)
                greeted += 1
    partner = gx + 1 - 2 * lax.rem(gx, 2)
    for step_y in range(1, n_gy):
        for friend_x in (gx, partner):
            friend = {"gx": friend_x, "gy": lax.rem(gy + step_y, n_gy)}
            pl.semaphore_signal(barrier, inc=1, device_id=friend, device_id_type=MESH)
            greeted += 1

    for copy in column_copies:
        copy.start()
    lax.fori_loop(0, planes, fetch, 0)
    courant_copy.start()

    tile_rows = tiles * LANES
    for copy in column_copies:
        copy.wait()
    owners, lines, bands = owner_ids[...], line_ids[...], band_ids[...]
    column_count = meso.shape[1]
    places = jnp.right_shift(owners, 1) * tile_rows + lines
    column_waves = waves_of(places.astype(jnp.float32))
    entries = meso.shape[0]
    shifted = jnp.concatenate(
        [meso[...], jnp.zeros((ENTRIES - entries, column_count), jnp.float32)], axis=0
    )
    for bit in range(4):
        moved = pltpu.roll(shifted, ENTRIES - (1 << bit), 0)
        chosen = jnp.bitwise_and(jnp.right_shift(bands, bit), 1) == 1
        shifted = jnp.where(chosen, moved, shifted)
    sides = [
        shifted * jnp.where(jnp.bitwise_and(owners, 1) == side, col_weight[...], 0.0)
        for side in range(2)
    ]
    sums = dot_two(
        in_two(jnp.concatenate(sides, axis=0)), in_two(column_waves), ((1,), (1,))
    )
    sum_send[0] = sums[:ENTRIES]
    sum_send[1] = sums[ENTRIES:]

    pl.semaphore_wait(barrier, greeted)

    def sum_copy(side, half_z):
        return pltpu.make_async_remote_copy(
            src_ref=sum_send.at[side, pl.ds(BAND_STEP * half_z, BAND_ROWS), :],
            dst_ref=sum_recv.at[2 * gx + gz],
            send_sem=ss_sem.at[side, half_z],
            recv_sem=sr_sem.at[2 * gx + gz],
            device_id={"gx": side * (n_gx - 1), "gz": half_z},
            device_id_type=MESH,
        )

    def each_sum(act, act_here):
        for side in range(2):
            for half_z in range(2):
                here = jnp.logical_and(gx == side * (n_gx - 1), gz == half_z)

                @pl.when(jnp.logical_not(here))
                def _():
                    act(sum_copy(side, half_z))

                if act_here is not None:

                    @pl.when(here)
                    def _():
                        act_here(side, half_z)

    def keep_sum(side, half_z):
        start = BAND_STEP * half_z
        sum_recv[2 * gx + gz] = sum_send[side, start : start + BAND_ROWS, :]

    each_sum(lambda copy: copy.start(), keep_sum)

    row_places = lax.broadcasted_iota(jnp.int32, (1, tile_rows), 1) + gy * tile_rows
    row_waves = waves_of(row_places.astype(jnp.float32))
    for piece, values in enumerate(in_two(row_waves)):
        waves_back[piece * 2 * KM : (piece + 1) * 2 * KM, :] = values
    for piece, values in enumerate(in_two(row_waves.T)):
        waves_to[piece] = values

    zero_rows = pl.ds(pl.multiple_of(jnp.where(gz == 0, 0, ROWS + levels), ROWS), ROWS)

    def blank(tile, carry):
        for state in (state_a, state_b):
            state[tile + tiles, zero_rows, :] = jnp.zeros((ROWS, LANES), jnp.float32)
        return carry

    lax.fori_loop(0, planes, blank, 0)
    y_send[...] = jnp.zeros_like(y_send)
    lane = lax.broadcasted_iota(jnp.int32, (ROWS, LANES), 1)

    whole = state_a.at[pl.ds(tiles, planes), body_rows, :]
    pltpu.make_async_copy(whole, whole, in_sem.at[0]).wait()

    part_rows = levels // 2

    def x_copy(step, side, piece):
        target = jnp.where(side == 0, x_right, x_left)
        return pltpu.make_async_remote_copy(
            src_ref=x_send.at[step, side, piece],
            dst_ref=x_recv.at[step, side, piece],
            send_sem=xs_sem.at[step, side, piece],
            recv_sem=xr_sem.at[step, side, piece],
            device_id={"gx": target},
            device_id_type=MESH,
        )

    def send_face(state, step, side, piece):
        base = ((1 - side) * (CX - 1) + 1) * tiles
        rows = pl.ds(ROWS + piece * part_rows, part_rows)
        for tile in range(tiles):
            x_send[step, side, piece, tile] = state[base + tile, rows, :].astype(jnp.bfloat16)
        x_copy(step, side, piece).start()

    def send_faces(side):
        for piece in range(2):
            send_face(state_a, 0, side, piece)

    @pl.when(jnp.logical_not(east_end))
    def _():
        send_faces(0)

    @pl.when(jnp.logical_not(west_end))
    def _():
        send_faces(1)

    fringe = jnp.logical_or(west_end, east_end)
    first = jnp.where(east_end, CX - FW, 0)
    end_x = jnp.where(fringe, gx, partner)
    helper_x = jnp.where(fringe, partner, gx)
    my_plane = jnp.where(fringe, gy, n_gy + gy)

    def part_copy(owner, peer):
        plane = peer + owner * n_gy
        return pltpu.make_async_remote_copy(
            src_ref=part.at[plane],
            dst_ref=part_recv.at[gy],
            send_sem=ps_sem.at[plane],
            recv_sem=pr_sem.at[gy],
            device_id={"gx": helper_x if owner else end_x, "gy": peer},
            device_id_type=MESH,
        )

    def part_arrival(source):
        return pltpu.make_async_remote_copy(
            src_ref=part.at[0],
            dst_ref=part_recv.at[source],
            send_sem=ps_sem.at[0],
            recv_sem=pr_sem.at[source],
            device_id={"gx": partner},
            device_id_type=MESH,
        )

    def coef_copy(peer):
        return pltpu.make_async_remote_copy(
            src_ref=coef.at[my_plane],
            dst_ref=coef.at[my_plane],
            send_sem=cs_sem.at[peer],
            recv_sem=cr_sem.at[my_plane],
            device_id={"gx": end_x, "gy": peer},
            device_id_type=MESH,
        )

    def coef_arrival(plane):
        return pltpu.make_async_remote_copy(
            src_ref=coef.at[plane],
            dst_ref=coef.at[plane],
            send_sem=cs_sem.at[0],
            recv_sem=cr_sem.at[plane],
            device_id={"gx": partner},
            device_id_type=MESH,
        )

    def scaled(total):
        mode = lax.broadcasted_iota(jnp.int32, (levels, 2 * KM), 1)
        scale = jnp.where(jnp.bitwise_and(mode, KM - 1) == 0, 1.0 / NY, 2.0 / NY)
        steps = jnp.where(end_x == 0, FW - my_plane, my_plane + 1).astype(jnp.float32)
        coef[my_plane] = (total * (scale * (steps * (1.0 / FW)))).astype(jnp.bfloat16)

    peers = [lax.rem(gy + step_y, n_gy) for step_y in range(1, n_gy)]

    @pl.when(fringe)
    def _():
        def strip_spectrum(index, carry):
            base = (first + index + 1) * tiles
            strip = jnp.concatenate(
                [state_a[base + tile, body_rows, :] for tile in range(tiles)], axis=1
            )
            at = pl.ds(pl.multiple_of(index * levels, levels), levels)
            for piece, values in enumerate(in_two(strip)):
                strips[piece, at, :] = values
            return carry

        lax.fori_loop(0, FW, strip_spectrum, 0)
        spectrum = dot_two(
            (strips[0], strips[1]), (waves_to[0], waves_to[1]), ((1,), (0,))
        )
        part[...] = spectrum.reshape(part.shape)

        total = jnp.zeros((BAND_ROWS, 2 * KM), jnp.float32)
        for slot in range(2 * n_gx):

            @pl.when(slot != 2 * gx + gz)
            def _():
                pltpu.make_async_remote_copy(
                    src_ref=sum_send.at[0, pl.ds(0, BAND_ROWS), :],
                    dst_ref=sum_recv.at[slot],
                    send_sem=ss_sem.at[0, 0],
                    recv_sem=sr_sem.at[slot],
                    device_id={"gz": other},
                    device_id_type=MESH,
                ).wait_recv()

        for slot in range(2 * n_gx):
            total = total + sum_recv[slot]
        level = lax.broadcasted_iota(jnp.int32, (levels, BAND_ROWS), 0) + gz * levels
        entry = lax.broadcasted_iota(jnp.int32, (levels, BAND_ROWS), 1) + gz * BAND_STEP
        lower = jnp.right_shift(3 * level, 3)
        fraction = jnp.bitwise_and(3 * level, 7).astype(jnp.float32) * 0.125
        band = jnp.where(entry == lower, 1.0 - fraction, 0.0) + jnp.where(
            entry == lower + 1, fraction, 0.0
        )
        target = jnp.dot(band, total, precision=highest, preferred_element_type=jnp.float32)

        def subtract(index, carry):
            part[index] = target - part[index]
            return carry

        lax.fori_loop(0, FW, subtract, 0)
        for peer in peers:
            part_copy(0, peer).start()
            part_copy(1, peer).start()
        part_copy(1, gy).start()

    courant_copy.wait()

    def weigh(tile, carry):
        centre = 1.0
        for direction in range(3):
            number = courant[direction, :, tile_lanes(tile)].astype(jnp.float32)
            upward = jnp.maximum(number, 0.0)
            behind = upward + diffusion
            ahead = (upward - number) + diffusion
            weight[2 * direction + 1, tile] = behind
            weight[2 * direction + 2, tile] = ahead
            centre = centre - (behind + ahead)
        weight[0, tile] = centre
        return carry

    lax.fori_loop(0, planes, weigh, 0)

    @pl.when(fringe)
    def _():
        for peer in peers:
            part_arrival(peer).wait_recv()
        total = part[gy]
        for peer in peers:
            total = total + part_recv[peer]
        scaled(total)
        for peer in peers:
            coef_copy(peer).start()
        for peer in peers:
            coef_arrival(peer).wait_recv()
        for peer in range(n_gy):
            coef_arrival(n_gy + peer).wait_recv()

        both = coef[...].reshape(FW * levels, 2 * KM)
        both = jnp.concatenate([both, both], axis=1)
        for start in range(0, tiles, 2):
            stop = min(start + 2, tiles)
            smooth = jnp.dot(
                both,
                waves_back[:, start * LANES : stop * LANES],
                preferred_element_type=jnp.float32,
            )
            for index in range(FW):
                own = slice(index * levels, (index + 1) * levels)
                for tile in range(start, stop):
                    at = (first + index + 1) * tiles + tile
                    where = slice((tile - start) * LANES, (tile - start + 1) * LANES)
                    state_a[at, body_rows, :] += smooth[own, where]

    @pl.when(jnp.logical_not(fringe))
    def _():
        for peer in range(n_gy):
            part_arrival(peer).wait_recv()
        total = part_recv[0]
        for peer in range(1, n_gy):
            total = total + part_recv[peer]
        scaled(total)
        for peer in range(n_gy):
            coef_copy(peer).start()

    @pl.when(east_end)
    def _():
        send_faces(0)

    @pl.when(west_end)
    def _():
        send_faces(1)

    source_rows = pl.ds(pl.multiple_of(jnp.where(gz == 0, levels, ROWS), ROWS), ROWS)
    target_rows = pl.ds(pl.multiple_of(jnp.where(gz == 0, 0, ROWS + levels), ROWS), ROWS)

    def z_copy(state, step, group):
        first, count = groups[group]
        some = pl.ds((first + 1) * tiles, count * tiles)
        return pltpu.make_async_remote_copy(
            src_ref=state.at[some, source_rows, :],
            dst_ref=state.at[some, target_rows, :],
            send_sem=zs_sem.at[step, group],
            recv_sem=zr_sem.at[step, group],
            device_id={"gz": other},
            device_id_type=MESH,
        )

    def y_copy(step, group, side):
        return pltpu.make_async_remote_copy(
            src_ref=y_send.at[step, group, side],
            dst_ref=y_recv.at[step, group, side],
            send_sem=ys_sem.at[step, group, side],
            recv_sem=yr_sem.at[step, group, side],
            device_id={"gy": y_right if side == 0 else y_left},
            device_id_type=MESH,
        )

    half = (CX - 2) // 2
    groups = ((1, half), (1 + half, half), (0, 1), (CX - 1, 1))

    def pack(step, group, plane, edges):
        right, left = y_send[step, group, 0], y_send[step, group, 1]
        for chunk, low, high in edges:
            place = plane + chunk * CX
            here = lane == place
            right = jnp.where(here, pltpu.roll(high, lax.rem(place + 1, LANES), 1), right)
            left = jnp.where(here, pltpu.roll(low, place, 1), left)
        y_send[step, group, 0] = right
        y_send[step, group, 1] = left

    def send(state, step, group):
        z_copy(state, step, group).start()
        for side in range(2):
            y_copy(step, group, side).start()

    def pack_planes(group):
        first_plane, count = groups[group]

        def pack_start(plane, carry):
            base = (plane + 1) * tiles
            edges = []
            for chunk in range(chunks):
                rows = pl.ds(ROWS + chunk * ROWS, ROWS)
                edges.append((chunk, state_a[base, rows, :], state_a[base + tiles - 1, rows, :]))
            pack(0, group, plane, edges)
            return carry

        lax.fori_loop(first_plane, first_plane + count, pack_start, 0)
        send(state_a, 0, group)

    for group in range(4):
        pack_planes(group)

    def advance(step, now, later, final):
        going_on = step < NSTEP - 1

        def arrive(group):
            z_copy(now, step, group).wait_recv()
            for side in range(2):
                y_copy(step, group, side).wait_recv()

            @pl.when(step > 0)
            def _():
                z_copy(later, step - 1, group).wait_send()

        def send_next(group):
            @pl.when(going_on)
            def _():
                send(later, step + 1, group)

        def move(plane, group, some):
            base = (plane + 1) * tiles
            from_left = y_recv[step, group, 0]
            from_right = y_recv[step, group, 1]
            edges = []
            for chunk in some:
                row = ROWS + chunk * ROWS
                rows = pl.ds(row, ROWS)
                own = pl.ds(chunk * ROWS, ROWS)
                place = plane + chunk * CX
                cells = [now[base + tile, rows, :] for tile in range(tiles)]
                up = [pltpu.roll(from_left, lax.rem(LANES - place, LANES), 1)]
                up = up + [pltpu.roll(cell, 1, 1) for cell in cells]
                down = [pltpu.roll(cell, LANES - 1, 1) for cell in cells]
                down = down + [pltpu.roll(from_right, LANES - 1 - place, 1)]
                results = []
                for tile in range(tiles):
                    at = base + tile
                    mine = plane * tiles + tile
                    near = (
                        cells[tile],
                        now[at - tiles, rows, :],
                        now[at + tiles, rows, :],
                        now[at, pl.ds(row - 1, ROWS), :],
                        now[at, pl.ds(row + 1, ROWS), :],
                        jnp.where(lane == 0, up[tile], up[tile + 1]),
                        jnp.where(lane == LANES - 1, down[tile + 1], down[tile]),
                    )
                    terms = [weight[k, mine, own, :] * near[k] for k in range(7)]
                    total = ((terms[1] + terms[2]) + (terms[3] + terms[4])) + (
                        (terms[5] + terms[6]) + terms[0]
                    )
                    later[at, rows, :] = total
                    if final:
                        out_ref[own, tile_lanes(mine)] = total
                    results.append(total)
                edges.append((chunk, results[0], results[-1]))
            pack(step + 1, group, plane, edges)

        for piece in range(2):
            arrive(piece)
            first_plane, count = groups[piece]

            def inner(plane, carry):
                move(plane, piece, range(chunks))
                return carry

            lax.fori_loop(first_plane, first_plane + count, inner, 0)
            send_next(piece)
            if piece == 0:
                arrive(2)
                arrive(3)
            some = range(piece * chunks // 2, (piece + 1) * chunks // 2)
            rows = pl.ds(ROWS + piece * part_rows, part_rows)

            def edge(end, carry):
                plane = end * (CX - 1)
                x_copy(step, end, piece).wait_recv()
                base = end * (CX + 1) * tiles
                for tile in range(tiles):
                    now[base + tile, rows, :] = x_recv[step, end, piece, tile].astype(jnp.float32)
                move(plane, 2 + end, some)

                @pl.when(going_on)
                def _():
                    send_face(later, step + 1, 1 - end, piece)

                return carry

            lax.fori_loop(0, 2, edge, 0)
        send_next(2)
        send_next(3)

    def two(pair, carry):
        advance(2 * pair, state_a, state_b, False)
        advance(2 * pair + 1, state_b, state_a, True)
        return carry

    lax.fori_loop(0, NSTEP // 2, two, 0)

    for group in range(4):
        z_copy(state_b, NSTEP - 1, group).wait_send()

    def settle(step, carry):
        for side in range(2):
            for piece in range(2):
                x_copy(step, side, piece).wait_send()
            for group in range(4):
                y_copy(step, group, side).wait_send()
        return carry

    lax.fori_loop(0, NSTEP, settle, 0)
    each_sum(lambda copy: copy.wait_send(), None)

    @pl.when(fringe)
    def _():
        for peer in peers:
            part_copy(0, peer).wait_send()
            part_copy(1, peer).wait_send()
            coef_copy(peer).wait_send()
        part_copy(1, gy).wait_send()

    @pl.when(jnp.logical_not(fringe))
    def _():
        for peer in range(n_gy):
            coef_copy(peer).wait_send()


def fast_sweep(theta, courants, meso, col_weight, owner, line, band, n_gx, n_gy, tile_rows):
    levels = theta.shape[0]
    tiles = tile_rows // LANES
    planes = CX * tiles
    slots = (CX + 2) * tiles
    f32, bf16 = jnp.float32, jnp.bfloat16
    field = pltpu.VMEM((slots, levels + 2 * ROWS, LANES), f32)
    faces = pltpu.VMEM((NSTEP, 2, 2, tiles, levels // 2, LANES), bf16)
    lines = pltpu.VMEM((NSTEP + 1, 4, 2, ROWS, LANES), f32)
    dma = pltpu.SemaphoreType.DMA
    main_memory = pl.BlockSpec(memory_space=pltpu.HBM)
    return pl.pallas_call(
        functools.partial(sweep_kernel, (n_gx, n_gy, levels, tiles)),
        out_shape=pltpu.VMEM(theta.shape, f32),
        in_specs=[main_memory] * 7,
        out_specs=pl.BlockSpec(memory_space=pltpu.VMEM),
        scratch_shapes=[
            field,
            field,
            pltpu.VMEM((7, planes, levels, LANES), f32),
            pltpu.VMEM(courants.shape, bf16),
            pltpu.VMEM(meso.shape, f32),
            pltpu.VMEM(col_weight.shape, f32),
            pltpu.VMEM(owner.shape, jnp.int32),
            pltpu.VMEM(line.shape, jnp.int32),
            pltpu.VMEM(band.shape, jnp.int32),
            pltpu.VMEM((2, tile_rows, 2 * KM), bf16),
            pltpu.VMEM((4 * KM, tile_rows), bf16),
            pltpu.VMEM((2, FW * levels, tile_rows), bf16),
            pltpu.VMEM((2, ENTRIES, 2 * KM), f32),
            pltpu.VMEM((2 * n_gx, BAND_ROWS, 2 * KM), f32),
            pltpu.VMEM((FW, levels, 2 * KM), f32),
            pltpu.VMEM((n_gy, levels, 2 * KM), f32),
            pltpu.VMEM((FW, levels, 2 * KM), bf16),
            faces,
            faces,
            lines,
            lines,
            dma((7,)),
            dma((NSTEP, 2, 2)),
            dma((NSTEP, 2, 2)),
            dma((NSTEP, 4, 2)),
            dma((NSTEP, 4, 2)),
            dma((NSTEP, 4)),
            dma((NSTEP, 4)),
            dma((2, 2)),
            dma((2 * n_gx,)),
            dma((FW,)),
            dma((n_gy,)),
            dma((n_gy,)),
            dma((FW,)),
        ],
        compiler_params=pltpu.CompilerParams(
            collective_id=0, has_side_effects=True, vmem_limit_bytes=48 * 1024 * 1024
        ),
        name="transport",
    )(theta, courants, meso, col_weight, owner, line, band)


def body(theta_field, courants, meso_columns, col_weight, owner_ids, line_ids, band_start):
    n_gx, n_gy, n_gz = (lax.axis_size(axis) for axis in ("gx", "gy", "gz"))
    tile_rows = NY // n_gy
    levels = theta_field.shape[2]
    theta_local = theta_field.reshape(levels, CX * tile_rows)
    courant_local = courants.reshape(3, levels, CX * tile_rows)
    column_index = lax.axis_index("gx")
    east_end = column_index == n_gx - 1
    west_end = column_index == 0

    fits = tile_rows % LANES == 0 and levels == 64 and FW == 2 * n_gy
    if fits and n_gz == 2 and n_gx == 4 and n_gy > 2:
        result = fast_sweep(
            theta_local,
            courant_local,
            meso_columns,
            col_weight[None, :],
            owner_ids.reshape(1, -1),
            line_ids[None, :],
            band_start[None, :],
            n_gx,
            n_gy,
            tile_rows,
        )
        return result.reshape(1, 1, levels, CX * tile_rows)

    sums = target_spectrum(meso_columns, col_weight, owner_ids, line_ids, band_start, tile_rows)
    sums = lax.psum(sums, ("gx", "gy", "gz"))
    side_sums = jnp.where(east_end, sums[:, 2 * KM :], sums[:, : 2 * KM])
    bands = lax.dynamic_slice_in_dim(band_matrix(), lax.axis_index("gz") * levels, levels, axis=0)
    target = jnp.dot(bands, side_sums, precision=highest, preferred_element_type=jnp.float32)

    own_waves = waves_at(lax.axis_index("gy") * tile_rows + jnp.arange(tile_rows, dtype=jnp.int32))
    width = FW * tile_rows
    strip = jnp.where(east_end, theta_local[:, -width:], theta_local[:, :width])
    strip = strip.reshape(levels, FW, tile_rows).transpose(1, 0, 2)
    spectrum = jnp.einsum(
        "xky,ym->xkm", strip, own_waves, precision=highest, preferred_element_type=jnp.float32
    )
    spectrum = target[None] - lax.psum(spectrum, "gy")
    offsets = jnp.arange(FW, dtype=jnp.float32)
    relaxation = jnp.where(
        east_end, (offsets + 1.0) / FW, jnp.where(west_end, (FW - offsets) / FW, 0.0)
    )
    coef = spectrum * mode_scale()[None, None, :] * relaxation[:, None, None]

    update = jnp.einsum(
        "xkm,ym->kxy", coef, own_waves, precision=highest, preferred_element_type=jnp.float32
    )
    state_field = theta_local.reshape(levels, CX, tile_rows)
    state_field = jnp.where(
        east_end,
        state_field.at[:, CX - FW :].add(update),
        state_field.at[:, :FW].add(update),
    )
    courant_field = courant_local.reshape(3, levels, CX, tile_rows)
    for step_index in range(NSTEP):
        state_field = sweep_once(state_field, courant_field)
    return state_field.reshape(1, 1, levels, CX * tile_rows)


def solution(mesh):
    in_specs = (
        P("gx", "gy", "gz", None),
        P(None, "gx", "gy", "gz", None),
        P(None, ("gx", "gy", "gz")),
        P(("gx", "gy", "gz")),
        P(("gx", "gy", "gz"), None),
        P(("gx", "gy", "gz")),
        P(("gx", "gy", "gz")),
    )
    out_specs = P("gx", "gy", "gz", None)
    return jax.shard_map(body, mesh=mesh, in_specs=in_specs, out_specs=out_specs, check_vma=False)
```

```python
import functools
import math

import jax
import jax.numpy as jnp
from jax import lax
from jax.experimental import pallas as pl
from jax.experimental.pallas import tpu as pltpu
from jax.sharding import PartitionSpec as P

CX = 16
NY = 3072
ZG = 128
KM = 64
FW = 8
NSTEP = 4
LANES = 128
ROWS = 8

MESH = pl.DeviceIdType.MESH
diffusion = 0.02
highest = lax.Precision.HIGHEST
band_span = 3 * (ZG - 1) // 8 + 2
ENTRIES = 64
BAND_STEP = 24
BAND_ROWS = 32


def extended(array, sides, width, wrap):
    for axis, dim in sides:
        devices, length = (lax.axis_size(axis), array.shape[dim])
        up = [(i, (i + 1) % devices) for i in range(devices if wrap else devices - 1)]
        down = [(j, i) for i, j in up]
        last = lax.slice_in_dim(array, length - width, length, axis=dim)
        initial = lax.slice_in_dim(array, 0, width, axis=dim)
        before = lax.ppermute(last, axis, up)
        after = lax.ppermute(initial, axis, down)
        array = jnp.concatenate([before, array, after], axis=dim)
    return array


def band_matrix():
    levels_z = jnp.arange(ZG, dtype=jnp.int32)
    lower_index = 3 * levels_z // 8
    fraction = (3 * levels_z % 8).astype(jnp.float32) / 8.0
    entries = jnp.arange(band_span, dtype=jnp.int32)[None, :]
    return (1.0 - fraction)[:, None] * (entries == lower_index[:, None]) + fraction[:, None] * (
        entries == lower_index[:, None] + 1
    )


def waves_at(places):
    numbers = jnp.arange(KM, dtype=jnp.int32)
    phases = places[:, None] * numbers[None, :] % NY
    angles = phases.astype(jnp.float32) * (2.0 * math.pi / NY)
    return jnp.concatenate([jnp.cos(angles), jnp.sin(angles)], axis=1)


def mode_scale():
    return jnp.where(jnp.arange(2 * KM, dtype=jnp.int32) % KM == 0, 1.0 / NY, 2.0 / NY).astype(
        jnp.float32
    )


def upwind(state_field, courant_one, ahead_cell, behind_cell):
    return -jnp.maximum(courant_one, 0.0) * (state_field - behind_cell) - jnp.minimum(
        courant_one, 0.0
    ) * (ahead_cell - state_field)


def sweep_once(state_field, courant_local):
    side_cells = extended(state_field, (("gx", 1), ("gy", 2)), 1, True)
    level_cells = extended(state_field, (("gz", 0),), 1, False)
    pairs = (
        (side_cells[:, 2:, 1:-1], side_cells[:, :-2, 1:-1]),
        (level_cells[2:], level_cells[:-2]),
        (side_cells[:, 1:-1, 2:], side_cells[:, 1:-1, :-2]),
    )
    change = 0.0
    neighbours = 0.0
    for direction, (ahead, behind) in enumerate(pairs):
        change = change + upwind(
            state_field, courant_local[direction].astype(jnp.float32), ahead, behind
        )
        neighbours = neighbours + ahead + behind
    return state_field + change + diffusion * (neighbours - 6.0 * state_field)


def target_spectrum(meso_columns, col_weight, owner_ids, line_ids, band_start, tile_rows):
    owners = owner_ids[:, 0]
    places = owners // 2 * tile_rows + line_ids
    waves = waves_at(places) * col_weight[:, None]
    sided = jnp.concatenate(
        [jnp.where((owners % 2 == side)[:, None], waves, 0.0) for side in range(2)], axis=1
    )
    shifted = jnp.zeros((band_span, meso_columns.shape[1]), jnp.float32)
    for offset in range(meso_columns.shape[0] - band_span + 1):
        shifted = shifted + jnp.where(
            band_start[None, :] == offset, meso_columns[offset : offset + band_span], 0.0
        )
    return jnp.dot(shifted, sided, precision=highest, preferred_element_type=jnp.float32)


def waves_of(places):
    numbers = lax.broadcasted_iota(jnp.int32, (KM, places.shape[1]), 0).astype(jnp.float32)
    turns = numbers * places
    quarter = NY // 4
    quarters = jnp.floor(turns * (1.0 / quarter) + 0.5)
    angle = (turns - quarter * quarters) * (2.0 * math.pi / NY)
    square = angle * angle
    sine = 1.0 / 362880.0
    for factor in (-1.0 / 5040.0, 1.0 / 120.0, -1.0 / 6.0, 1.0):
        sine = sine * square + factor
    sine = sine * angle
    cosine = 1.0 / 40320.0
    for factor in (-1.0 / 720.0, 1.0 / 24.0, -0.5, 1.0):
        cosine = cosine * square + factor
    corner = quarters - 4.0 * jnp.floor(quarters * 0.25)
    odd = jnp.logical_or(corner == 1.0, corner == 3.0)
    cos_values = jnp.where(odd, sine, cosine)
    sin_values = jnp.where(odd, cosine, sine)
    cos_values = jnp.where(
        jnp.logical_or(corner == 1.0, corner == 2.0), -cos_values, cos_values
    )
    sin_values = jnp.where(corner >= 2.0, -sin_values, sin_values)
    return jnp.concatenate([cos_values, sin_values], axis=0)


def in_two(values):
    high = values.astype(jnp.bfloat16)
    return high, (values - high.astype(jnp.float32)).astype(jnp.bfloat16)


def dot_two(left, right, dims):
    def one(a, b):
        return lax.dot_general(a, b, (dims, ((), ())), preferred_element_type=jnp.float32)

    return one(left[0], right[0]) + (one(left[1], right[0]) + one(left[0], right[1]))


def sweep_kernel(
    sizes,
    theta_ref,
    courant_ref,
    meso_ref,
    col_weight_ref,
    owner_ref,
    line_ref,
    band_ref,
    out_ref,
    state_a,
    state_b,
    weight,
    courant,
    meso,
    col_weight,
    owner_ids,
    line_ids,
    band_ids,
    waves_to,
    waves_back,
    strips,
    sum_send,
    sum_recv,
    part,
    part_recv,
    coef,
    x_send,
    x_recv,
    y_send,
    y_recv,
    in_sem,
    xs_sem,
    xr_sem,
    ys_sem,
    yr_sem,
    zs_sem,
    zr_sem,
    ss_sem,
    sr_sem,
    ps_sem,
    pr_sem,
    cs_sem,
    cr_sem,
):
    n_gx, n_gy, levels, tiles = sizes
    chunks = levels // ROWS
    planes = CX * tiles
    gx, gy, gz = (lax.axis_index(axis) for axis in ("gx", "gy", "gz"))
    x_right, x_left = lax.rem(gx + 1, n_gx), lax.rem(gx + n_gx - 1, n_gx)
    y_right, y_left = lax.rem(gy + 1, n_gy), lax.rem(gy + n_gy - 1, n_gy)
    other = 1 - gz
    east_end = gx == n_gx - 1
    west_end = gx == 0
    body_rows = pl.ds(ROWS, levels)

    def tile_lanes(tile):
        return pl.ds(pl.multiple_of(tile * LANES, LANES), LANES)

    courant_copy = pltpu.make_async_copy(courant_ref, courant, in_sem.at[1])
    column_copies = [
        pltpu.make_async_copy(meso_ref, meso, in_sem.at[2]),
        pltpu.make_async_copy(col_weight_ref, col_weight, in_sem.at[3]),
        pltpu.make_async_copy(owner_ref, owner_ids, in_sem.at[4]),
        pltpu.make_async_copy(line_ref, line_ids, in_sem.at[5]),
        pltpu.make_async_copy(band_ref, band_ids, in_sem.at[6]),
    ]

    def fetch(tile, carry):
        pltpu.make_async_copy(
            theta_ref.at[:, tile_lanes(tile)],
            state_a.at[tile + tiles, body_rows, :],
            in_sem.at[0],
        ).start()
        return carry

    barrier = pltpu.get_barrier_semaphore()
    greeted = 0
    for step_x in range(n_gx):
        for step_z in range(2):
            if step_x + step_z > 0:
                friend = {"gx": lax.rem(gx + step_x, n_gx), "gz": lax.rem(gz + step_z, 2)}
                pl.semaphore_signal(barrier, inc=1, device_id=friend, device_id_type=MESH)
                greeted += 1
    partner = gx + 1 - 2 * lax.rem(gx, 2)
    for step_y in range(1, n_gy):
        for friend_x in (gx, partner):
            friend = {"gx": friend_x, "gy": lax.rem(gy + step_y, n_gy)}
            pl.semaphore_signal(barrier, inc=1, device_id=friend, device_id_type=MESH)
            greeted += 1

    for copy in column_copies:
        copy.start()
    lax.fori_loop(0, planes, fetch, 0)
    courant_copy.start()

    tile_rows = tiles * LANES
    for copy in column_copies:
        copy.wait()
    owners, lines, bands = owner_ids[...], line_ids[...], band_ids[...]
    column_count = meso.shape[1]
    places = jnp.right_shift(owners, 1) * tile_rows + lines
    column_waves = waves_of(places.astype(jnp.float32))
    entries = meso.shape[0]
    shifted = jnp.concatenate(
        [meso[...], jnp.zeros((ENTRIES - entries, column_count), jnp.float32)], axis=0
    )
    for bit in range(4):
        moved = pltpu.roll(shifted, ENTRIES - (1 << bit), 0)
        chosen = jnp.bitwise_and(jnp.right_shift(bands, bit), 1) == 1
        shifted = jnp.where(chosen, moved, shifted)
    sides = [
        shifted * jnp.where(jnp.bitwise_and(owners, 1) == side, col_weight[...], 0.0)
        for side in range(2)
    ]
    sums = dot_two(
        in_two(jnp.concatenate(sides, axis=0)), in_two(column_waves), ((1,), (1,))
    )
    sum_send[0] = sums[:ENTRIES]
    sum_send[1] = sums[ENTRIES:]

    pl.semaphore_wait(barrier, greeted)

    def sum_copy(side, half_z):
        return pltpu.make_async_remote_copy(
            src_ref=sum_send.at[side, pl.ds(BAND_STEP * half_z, BAND_ROWS), :],
            dst_ref=sum_recv.at[2 * gx + gz],
            send_sem=ss_sem.at[side, half_z],
            recv_sem=sr_sem.at[2 * gx + gz],
            device_id={"gx": side * (n_gx - 1), "gz": half_z},
            device_id_type=MESH,
        )

    def each_sum(act, act_here):
        for side in range(2):
            for half_z in range(2):
                here = jnp.logical_and(gx == side * (n_gx - 1), gz == half_z)

                @pl.when(jnp.logical_not(here))
                def _():
                    act(sum_copy(side, half_z))

                if act_here is not None:

                    @pl.when(here)
                    def _():
                        act_here(side, half_z)

    def keep_sum(side, half_z):
        start = BAND_STEP * half_z
        sum_recv[2 * gx + gz] = sum_send[side, start : start + BAND_ROWS, :]

    each_sum(lambda copy: copy.start(), keep_sum)

    row_places = lax.broadcasted_iota(jnp.int32, (1, tile_rows), 1) + gy * tile_rows
    row_waves = waves_of(row_places.astype(jnp.float32))
    for piece, values in enumerate(in_two(row_waves)):
        waves_back[piece * 2 * KM : (piece + 1) * 2 * KM, :] = values
    for piece, values in enumerate(in_two(row_waves.T)):
        waves_to[piece] = values

    zero_rows = pl.ds(pl.multiple_of(jnp.where(gz == 0, 0, ROWS + levels), ROWS), ROWS)

    def blank(tile, carry):
        for state in (state_a, state_b):
            state[tile + tiles, zero_rows, :] = jnp.zeros((ROWS, LANES), jnp.float32)
        return carry

    lax.fori_loop(0, planes, blank, 0)
    y_send[...] = jnp.zeros_like(y_send)
    lane = lax.broadcasted_iota(jnp.int32, (ROWS, LANES), 1)

    whole = state_a.at[pl.ds(tiles, planes), body_rows, :]
    pltpu.make_async_copy(whole, whole, in_sem.at[0]).wait()

    part_rows = levels // 2

    def x_copy(step, side, piece):
        target = jnp.where(side == 0, x_right, x_left)
        return pltpu.make_async_remote_copy(
            src_ref=x_send.at[step, side, piece],
            dst_ref=x_recv.at[step, side, piece],
            send_sem=xs_sem.at[step, side, piece],
            recv_sem=xr_sem.at[step, side, piece],
            device_id={"gx": target},
            device_id_type=MESH,
        )

    def send_face(state, step, side, piece):
        base = ((1 - side) * (CX - 1) + 1) * tiles
        rows = pl.ds(ROWS + piece * part_rows, part_rows)
        for tile in range(tiles):
            x_send[step, side, piece, tile] = state[base + tile, rows, :].astype(jnp.bfloat16)
        x_copy(step, side, piece).start()

    def send_faces(side):
        for piece in range(2):
            send_face(state_a, 0, side, piece)

    @pl.when(jnp.logical_not(east_end))
    def _():
        send_faces(0)

    @pl.when(jnp.logical_not(west_end))
    def _():
        send_faces(1)

    fringe = jnp.logical_or(west_end, east_end)
    first = jnp.where(east_end, CX - FW, 0)
    end_x = jnp.where(fringe, gx, partner)
    helper_x = jnp.where(fringe, partner, gx)
    my_plane = jnp.where(fringe, gy, n_gy + gy)

    def part_copy(owner, peer):
        plane = peer + owner * n_gy
        return pltpu.make_async_remote_copy(
            src_ref=part.at[plane],
            dst_ref=part_recv.at[gy],
            send_sem=ps_sem.at[plane],
            recv_sem=pr_sem.at[gy],
            device_id={"gx": helper_x if owner else end_x, "gy": peer},
            device_id_type=MESH,
        )

    def part_arrival(source):
        return pltpu.make_async_remote_copy(
            src_ref=part.at[0],
            dst_ref=part_recv.at[source],
            send_sem=ps_sem.at[0],
            recv_sem=pr_sem.at[source],
            device_id={"gx": partner},
            device_id_type=MESH,
        )

    def coef_copy(peer):
        return pltpu.make_async_remote_copy(
            src_ref=coef.at[my_plane],
            dst_ref=coef.at[my_plane],
            send_sem=cs_sem.at[peer],
            recv_sem=cr_sem.at[my_plane],
            device_id={"gx": end_x, "gy": peer},
            device_id_type=MESH,
        )

    def coef_arrival(plane):
        return pltpu.make_async_remote_copy(
            src_ref=coef.at[plane],
            dst_ref=coef.at[plane],
            send_sem=cs_sem.at[0],
            recv_sem=cr_sem.at[plane],
            device_id={"gx": partner},
            device_id_type=MESH,
        )

    def scaled(total):
        mode = lax.broadcasted_iota(jnp.int32, (levels, 2 * KM), 1)
        scale = jnp.where(jnp.bitwise_and(mode, KM - 1) == 0, 1.0 / NY, 2.0 / NY)
        steps = jnp.where(end_x == 0, FW - my_plane, my_plane + 1).astype(jnp.float32)
        coef[my_plane] = (total * (scale * (steps * (1.0 / FW)))).astype(jnp.bfloat16)

    peers = [lax.rem(gy + step_y, n_gy) for step_y in range(1, n_gy)]

    @pl.when(fringe)
    def _():
        def strip_spectrum(index, carry):
            base = (first + index + 1) * tiles
            strip = jnp.concatenate(
                [state_a[base + tile, body_rows, :] for tile in range(tiles)], axis=1
            )
            at = pl.ds(pl.multiple_of(index * levels, levels), levels)
            for piece, values in enumerate(in_two(strip)):
                strips[piece, at, :] = values
            return carry

        lax.fori_loop(0, FW, strip_spectrum, 0)
        spectrum = dot_two(
            (strips[0], strips[1]), (waves_to[0], waves_to[1]), ((1,), (0,))
        )
        part[...] = spectrum.reshape(part.shape)

        total = jnp.zeros((BAND_ROWS, 2 * KM), jnp.float32)
        for slot in range(2 * n_gx):

            @pl.when(slot != 2 * gx + gz)
            def _():
                pltpu.make_async_remote_copy(
                    src_ref=sum_send.at[0, pl.ds(0, BAND_ROWS), :],
                    dst_ref=sum_recv.at[slot],
                    send_sem=ss_sem.at[0, 0],
                    recv_sem=sr_sem.at[slot],
                    device_id={"gz": other},
                    device_id_type=MESH,
                ).wait_recv()

        for slot in range(2 * n_gx):
            total = total + sum_recv[slot]
        level = lax.broadcasted_iota(jnp.int32, (levels, BAND_ROWS), 0) + gz * levels
        entry = lax.broadcasted_iota(jnp.int32, (levels, BAND_ROWS), 1) + gz * BAND_STEP
        lower = jnp.right_shift(3 * level, 3)
        fraction = jnp.bitwise_and(3 * level, 7).astype(jnp.float32) * 0.125
        band = jnp.where(entry == lower, 1.0 - fraction, 0.0) + jnp.where(
            entry == lower + 1, fraction, 0.0
        )
        target = jnp.dot(band, total, precision=highest, preferred_element_type=jnp.float32)

        def subtract(index, carry):
            part[index] = target - part[index]
            return carry

        lax.fori_loop(0, FW, subtract, 0)
        for peer in peers:
            part_copy(0, peer).start()
            part_copy(1, peer).start()
        part_copy(1, gy).start()

    courant_copy.wait()

    def weigh(tile, carry):
        centre = 1.0
        for direction in range(3):
            number = courant[direction, :, tile_lanes(tile)].astype(jnp.float32)
            upward = jnp.maximum(number, 0.0)
            behind = upward + diffusion
            ahead = (upward - number) + diffusion
            weight[2 * direction + 1, tile] = behind
            weight[2 * direction + 2, tile] = ahead
            centre = centre - (behind + ahead)
        weight[0, tile] = centre
        return carry

    lax.fori_loop(0, planes, weigh, 0)

    @pl.when(fringe)
    def _():
        for peer in peers:
            part_arrival(peer).wait_recv()
        total = part[gy]
        for peer in peers:
            total = total + part_recv[peer]
        scaled(total)
        for peer in peers:
            coef_copy(peer).start()
        for peer in peers:
            coef_arrival(peer).wait_recv()
        for peer in range(n_gy):
            coef_arrival(n_gy + peer).wait_recv()

        both = coef[...].reshape(FW * levels, 2 * KM)
        both = jnp.concatenate([both, both], axis=1)
        for start in range(0, tiles, 2):
            stop = min(start + 2, tiles)
            smooth = jnp.dot(
                both,
                waves_back[:, start * LANES : stop * LANES],
                preferred_element_type=jnp.float32,
            )
            for index in range(FW):
                own = slice(index * levels, (index + 1) * levels)
                for tile in range(start, stop):
                    at = (first + index + 1) * tiles + tile
                    where = slice((tile - start) * LANES, (tile - start + 1) * LANES)
                    state_a[at, body_rows, :] += smooth[own, where]

    @pl.when(jnp.logical_not(fringe))
    def _():
        for peer in range(n_gy):
            part_arrival(peer).wait_recv()
        total = part_recv[0]
        for peer in range(1, n_gy):
            total = total + part_recv[peer]
        scaled(total)
        for peer in range(n_gy):
            coef_copy(peer).start()

    @pl.when(east_end)
    def _():
        send_faces(0)

    @pl.when(west_end)
    def _():
        send_faces(1)

    source_rows = pl.ds(pl.multiple_of(jnp.where(gz == 0, levels, ROWS), ROWS), ROWS)
    target_rows = pl.ds(pl.multiple_of(jnp.where(gz == 0, 0, ROWS + levels), ROWS), ROWS)

    def z_copy(state, step, group):
        first, count = groups[group]
        some = pl.ds((first + 1) * tiles, count * tiles)
        return pltpu.make_async_remote_copy(
            src_ref=state.at[some, source_rows, :],
            dst_ref=state.at[some, target_rows, :],
            send_sem=zs_sem.at[step, group],
            recv_sem=zr_sem.at[step, group],
            device_id={"gz": other},
            device_id_type=MESH,
        )

    def y_copy(step, group, side):
        return pltpu.make_async_remote_copy(
            src_ref=y_send.at[step, group, side],
            dst_ref=y_recv.at[step, group, side],
            send_sem=ys_sem.at[step, group, side],
            recv_sem=yr_sem.at[step, group, side],
            device_id={"gy": y_right if side == 0 else y_left},
            device_id_type=MESH,
        )

    half = (CX - 2) // 2
    groups = ((1, half), (1 + half, half), (0, 1), (CX - 1, 1))

    def pack(step, group, plane, edges):
        right, left = y_send[step, group, 0], y_send[step, group, 1]
        for chunk, low, high in edges:
            place = plane + chunk * CX
            here = lane == place
            right = jnp.where(here, pltpu.roll(high, lax.rem(place + 1, LANES), 1), right)
            left = jnp.where(here, pltpu.roll(low, place, 1), left)
        y_send[step, group, 0] = right
        y_send[step, group, 1] = left

    def send(state, step, group):
        z_copy(state, step, group).start()
        for side in range(2):
            y_copy(step, group, side).start()

    def pack_planes(group):
        first_plane, count = groups[group]

        def pack_start(plane, carry):
            base = (plane + 1) * tiles
            edges = []
            for chunk in range(chunks):
                rows = pl.ds(ROWS + chunk * ROWS, ROWS)
                edges.append((chunk, state_a[base, rows, :], state_a[base + tiles - 1, rows, :]))
            pack(0, group, plane, edges)
            return carry

        lax.fori_loop(first_plane, first_plane + count, pack_start, 0)
        send(state_a, 0, group)

    for group in range(4):
        pack_planes(group)

    def advance(step, now, later, final):
        going_on = step < NSTEP - 1

        def arrive(group):
            z_copy(now, step, group).wait_recv()
            for side in range(2):
                y_copy(step, group, side).wait_recv()

            @pl.when(step > 0)
            def _():
                z_copy(later, step - 1, group).wait_send()

        def send_next(group):
            @pl.when(going_on)
            def _():
                send(later, step + 1, group)

        def move(plane, group, some):
            base = (plane + 1) * tiles
            from_left = y_recv[step, group, 0]
            from_right = y_recv[step, group, 1]
            edges = []
            for chunk in some:
                row = ROWS + chunk * ROWS
                rows = pl.ds(row, ROWS)
                own = pl.ds(chunk * ROWS, ROWS)
                place = plane + chunk * CX
                cells = [now[base + tile, rows, :] for tile in range(tiles)]
                up = [pltpu.roll(from_left, lax.rem(LANES - place, LANES), 1)]
                up = up + [pltpu.roll(cell, 1, 1) for cell in cells]
                down = [pltpu.roll(cell, LANES - 1, 1) for cell in cells]
                down = down + [pltpu.roll(from_right, LANES - 1 - place, 1)]
                results = []
                for tile in range(tiles):
                    at = base + tile
                    mine = plane * tiles + tile
                    near = (
                        cells[tile],
                        now[at - tiles, rows, :],
                        now[at + tiles, rows, :],
                        now[at, pl.ds(row - 1, ROWS), :],
                        now[at, pl.ds(row + 1, ROWS), :],
                        jnp.where(lane == 0, up[tile], up[tile + 1]),
                        jnp.where(lane == LANES - 1, down[tile + 1], down[tile]),
                    )
                    terms = [weight[k, mine, own, :] * near[k] for k in range(7)]
                    total = ((terms[1] + terms[2]) + (terms[3] + terms[4])) + (
                        (terms[5] + terms[6]) + terms[0]
                    )
                    later[at, rows, :] = total
                    if final:
                        out_ref[own, tile_lanes(mine)] = total
                    results.append(total)
                edges.append((chunk, results[0], results[-1]))
            pack(step + 1, group, plane, edges)

        for piece in range(2):
            arrive(piece)
            first_plane, count = groups[piece]

            def inner(plane, carry):
                move(plane, piece, range(chunks))
                return carry

            lax.fori_loop(first_plane, first_plane + count, inner, 0)
            send_next(piece)
            if piece == 0:
                arrive(2)
                arrive(3)
            some = range(piece * chunks // 2, (piece + 1) * chunks // 2)
            rows = pl.ds(ROWS + piece * part_rows, part_rows)

            def edge(end, carry):
                plane = end * (CX - 1)
                x_copy(step, end, piece).wait_recv()
                base = end * (CX + 1) * tiles
                for tile in range(tiles):
                    now[base + tile, rows, :] = x_recv[step, end, piece, tile].astype(jnp.float32)
                move(plane, 2 + end, some)

                @pl.when(going_on)
                def _():
                    send_face(later, step + 1, 1 - end, piece)

                return carry

            lax.fori_loop(0, 2, edge, 0)
        send_next(2)
        send_next(3)

    def two(pair, carry):
        advance(2 * pair, state_a, state_b, False)
        advance(2 * pair + 1, state_b, state_a, True)
        return carry

    lax.fori_loop(0, NSTEP // 2, two, 0)

    for group in range(4):
        z_copy(state_b, NSTEP - 1, group).wait_send()

    def settle(step, carry):
        for side in range(2):
            for piece in range(2):
                x_copy(step, side, piece).wait_send()
            for group in range(4):
                y_copy(step, group, side).wait_send()
        return carry

    lax.fori_loop(0, NSTEP, settle, 0)
    each_sum(lambda copy: copy.wait_send(), None)

    @pl.when(fringe)
    def _():
        for peer in peers:
            part_copy(0, peer).wait_send()
            part_copy(1, peer).wait_send()
            coef_copy(peer).wait_send()
        part_copy(1, gy).wait_send()

    @pl.when(jnp.logical_not(fringe))
    def _():
        for peer in range(n_gy):
            coef_copy(peer).wait_send()


def fast_sweep(theta, courants, meso, col_weight, owner, line, band, n_gx, n_gy, tile_rows):
    levels = theta.shape[0]
    tiles = tile_rows // LANES
    planes = CX * tiles
    slots = (CX + 2) * tiles
    f32, bf16 = jnp.float32, jnp.bfloat16
    field = pltpu.VMEM((slots, levels + 2 * ROWS, LANES), f32)
    faces = pltpu.VMEM((NSTEP, 2, 2, tiles, levels // 2, LANES), bf16)
    lines = pltpu.VMEM((NSTEP + 1, 4, 2, ROWS, LANES), f32)
    dma = pltpu.SemaphoreType.DMA
    main_memory = pl.BlockSpec(memory_space=pltpu.HBM)
    return pl.pallas_call(
        functools.partial(sweep_kernel, (n_gx, n_gy, levels, tiles)),
        out_shape=pltpu.VMEM(theta.shape, f32),
        in_specs=[main_memory] * 7,
        out_specs=pl.BlockSpec(memory_space=pltpu.VMEM),
        scratch_shapes=[
            field,
            field,
            pltpu.VMEM((7, planes, levels, LANES), f32),
            pltpu.VMEM(courants.shape, bf16),
            pltpu.VMEM(meso.shape, f32),
            pltpu.VMEM(col_weight.shape, f32),
            pltpu.VMEM(owner.shape, jnp.int32),
            pltpu.VMEM(line.shape, jnp.int32),
            pltpu.VMEM(band.shape, jnp.int32),
            pltpu.VMEM((2, tile_rows, 2 * KM), bf16),
            pltpu.VMEM((4 * KM, tile_rows), bf16),
            pltpu.VMEM((2, FW * levels, tile_rows), bf16),
            pltpu.VMEM((2, ENTRIES, 2 * KM), f32),
            pltpu.VMEM((2 * n_gx, BAND_ROWS, 2 * KM), f32),
            pltpu.VMEM((FW, levels, 2 * KM), f32),
            pltpu.VMEM((n_gy, levels, 2 * KM), f32),
            pltpu.VMEM((FW, levels, 2 * KM), bf16),
            faces,
            faces,
            lines,
            lines,
            dma((7,)),
            dma((NSTEP, 2, 2)),
            dma((NSTEP, 2, 2)),
            dma((NSTEP, 4, 2)),
            dma((NSTEP, 4, 2)),
            dma((NSTEP, 4)),
            dma((NSTEP, 4)),
            dma((2, 2)),
            dma((2 * n_gx,)),
            dma((FW,)),
            dma((n_gy,)),
            dma((n_gy,)),
            dma((FW,)),
        ],
        compiler_params=pltpu.CompilerParams(
            collective_id=0, has_side_effects=True, vmem_limit_bytes=58 * 1024 * 1024
        ),
        name="transport",
    )(theta, courants, meso, col_weight, owner, line, band)


def body(theta_field, courants, meso_columns, col_weight, owner_ids, line_ids, band_start):
    n_gx, n_gy, n_gz = (lax.axis_size(axis) for axis in ("gx", "gy", "gz"))
    tile_rows = NY // n_gy
    levels = theta_field.shape[2]
    theta_local = theta_field.reshape(levels, CX * tile_rows)
    courant_local = courants.reshape(3, levels, CX * tile_rows)
    column_index = lax.axis_index("gx")
    east_end = column_index == n_gx - 1
    west_end = column_index == 0

    fits = tile_rows % LANES == 0 and levels == 64 and FW == 2 * n_gy
    if fits and n_gz == 2 and n_gx == 4 and n_gy > 2:
        result = fast_sweep(
            theta_local,
            courant_local,
            meso_columns,
            col_weight[None, :],
            owner_ids.reshape(1, -1),
            line_ids[None, :],
            band_start[None, :],
            n_gx,
            n_gy,
            tile_rows,
        )
        return result.reshape(1, 1, levels, CX * tile_rows)

    sums = target_spectrum(meso_columns, col_weight, owner_ids, line_ids, band_start, tile_rows)
    sums = lax.psum(sums, ("gx", "gy", "gz"))
    side_sums = jnp.where(east_end, sums[:, 2 * KM :], sums[:, : 2 * KM])
    bands = lax.dynamic_slice_in_dim(band_matrix(), lax.axis_index("gz") * levels, levels, axis=0)
    target = jnp.dot(bands, side_sums, precision=highest, preferred_element_type=jnp.float32)

    own_waves = waves_at(lax.axis_index("gy") * tile_rows + jnp.arange(tile_rows, dtype=jnp.int32))
    width = FW * tile_rows
    strip = jnp.where(east_end, theta_local[:, -width:], theta_local[:, :width])
    strip = strip.reshape(levels, FW, tile_rows).transpose(1, 0, 2)
    spectrum = jnp.einsum(
        "xky,ym->xkm", strip, own_waves, precision=highest, preferred_element_type=jnp.float32
    )
    spectrum = target[None] - lax.psum(spectrum, "gy")
    offsets = jnp.arange(FW, dtype=jnp.float32)
    relaxation = jnp.where(
        east_end, (offsets + 1.0) / FW, jnp.where(west_end, (FW - offsets) / FW, 0.0)
    )
    coef = spectrum * mode_scale()[None, None, :] * relaxation[:, None, None]

    update = jnp.einsum(
        "xkm,ym->kxy", coef, own_waves, precision=highest, preferred_element_type=jnp.float32
    )
    state_field = theta_local.reshape(levels, CX, tile_rows)
    state_field = jnp.where(
        east_end,
        state_field.at[:, CX - FW :].add(update),
        state_field.at[:, :FW].add(update),
    )
    courant_field = courant_local.reshape(3, levels, CX, tile_rows)
    for step_index in range(NSTEP):
        state_field = sweep_once(state_field, courant_field)
    return state_field.reshape(1, 1, levels, CX * tile_rows)


def solution(mesh):
    in_specs = (
        P("gx", "gy", "gz", None),
        P(None, "gx", "gy", "gz", None),
        P(None, ("gx", "gy", "gz")),
        P(("gx", "gy", "gz")),
        P(("gx", "gy", "gz"), None),
        P(("gx", "gy", "gz")),
        P(("gx", "gy", "gz")),
    )
    out_specs = P("gx", "gy", "gz", None)
    return jax.shard_map(body, mesh=mesh, in_specs=in_specs, out_specs=out_specs, check_vma=False)
```
